512 devices in a mesh: seq: 64 (over x, y_hi, z), chan: 8 (over y_lo, core).
Axes of the slice: x: 4, y: 8 (y_hi: 2, y_lo: 4; y = y_hi * 4 + y_lo), z: 8, core: 2. Of those that a mesh axis runs over, the one named last changes fastest.
Arguments:
- inputs: bfloat16 [3, 256, 16384], P(None, 'chan', 'seq'), may hold values from -6 to 6
- short_weights: float32 [3, 3, 256], P(None, None, 'chan'), may hold values from -3 to 3
- filters: float32 [32, 16384], P(None, 'seq'), may hold values from -1.2 to 1.2
- skip: float32 [256], P('chan'), may hold values from -4 to 4
- grad_out: bfloat16 [256, 16384], P('chan', 'seq'), may hold values from -7.5 to 7.5
Outputs:
- input_grads: float32 [3, 256, 16384], P(None, 'chan', 'seq')
- filter_grad: float32 [32, 16384], P('chan', 'seq')
- skip_grad: float32 [256], P('chan')
- short_grad: float32 [3, 3, 256], P(None, None, 'chan')
The draws below stay inside these ranges and needn't reach their ends.
All inputs are finite; a program needn't handle non-finite values.
Results may differ from the reference program's by a relative error of at most 0.0003.
Values may be sent and summed in bfloat16 or wider, within the bound.
No kernel may reach another device: no remote copies, remote signals or barrier semaphores. Data moves between devices by JAX's collectives and lax.ppermute only.
A program may use at most 64 MiB of HBM per device.

```python
import jax
import jax.numpy as jnp
from jax import lax

KS = 3
SEQ = 16384
CHANNELS = 256
FILTERS = 32


def draw_filters(key, part):
    key = jax.random.fold_in(key, 11)
    first, second = jax.random.split(key)
    position = jnp.arange(SEQ, dtype=jnp.float32)[None, :]
    lowest, highest = (40.0, 4.0 * SEQ)
    spread = jax.random.uniform(first, (FILTERS, 1), jnp.float32)
    reach = jnp.exp(jnp.log(lowest) + spread * (jnp.log(highest) - jnp.log(lowest)))
    envelope = jnp.exp(-position / reach) * jnp.sqrt(2.0 / jnp.minimum(reach, 1.0 * SEQ))
    return envelope * jnp.clip(jax.random.normal(second, (FILTERS, SEQ), jnp.float32), -5.0, 5.0)


def draw_grad_out(key, part):
    key = jax.random.fold_in(key, 23)
    position = jnp.arange(SEQ, dtype=jnp.float32)[None, :] / SEQ
    values = jnp.clip(jax.random.normal(key, (CHANNELS, SEQ), jnp.float32), -5.0, 5.0)
    return (values * (0.5 + position)).astype(jnp.bfloat16)


def steps_of(rng, shape, shards, low, largest):
    def one(dim, shards_of):
        draws = jax.random.uniform(jax.random.fold_in(jax.random.fold_in(rng, 6), dim), (shards_of,), jnp.float32, low / len(shards), largest / len(shards))
        return jnp.repeat(jnp.exp(draws), shape[dim] // shards_of).reshape((-1,) + (1,) * (len(shape) - dim - 1))

    gain = one(*shards[0])
    for cut in shards[1:]:
        gain = gain * one(*cut)
    return gain


def bell_draw(own_key, extent, scale, limit, cuts=(), held_as=jnp.bfloat16):
    gain = steps_of(own_key, extent, cuts, -0.22, 0.18) if cuts else 1.0
    values = jax.random.normal(own_key, extent, jnp.float32) * scale * gain
    return jnp.minimum(jnp.maximum(values, -limit), limit).astype(held_as)


def setup_inputs(seed: int = 0) -> dict:
    seeds = jax.random.split(jax.random.key(seed), 6)
    inputs = bell_draw(seeds[0], (3, CHANNELS, SEQ), 1.0, 6.0, ((1, 8), (2, 64)))
    short_weights = bell_draw(seeds[1], (3, KS, CHANNELS), 0.6, 3.0, ((2, 8),), jnp.float32)
    filters = draw_filters(jax.random.fold_in(seeds[5], 71), 0)
    skip = bell_draw(seeds[3], (CHANNELS,), 0.8, 4.0, ((0, 8),), jnp.float32)
    grad_out = draw_grad_out(jax.random.fold_in(seeds[5], 71), 0)
    return {"inputs": inputs, "short_weights": short_weights, "filters": filters, "skip": skip, "grad_out": grad_out}


def causal_short(signal, taps):
    result = taps[0][:, None] * signal
    for offset in range(1, KS):
        moved = jnp.pad(signal, ((0, 0), (offset, 0)))[:, :-offset]
        result = result + taps[offset][:, None] * moved
    return result


def adjoint_short(gradient, taps):
    result = taps[0][:, None] * gradient
    for offset in range(1, KS):
        moved = jnp.pad(gradient, ((0, 0), (0, offset)))[:, offset:]
        result = result + taps[offset][:, None] * moved
    return result


def short_terms(gradient, signal):
    rows = [jnp.sum(gradient * signal, axis=1)]
    for offset in range(1, KS):
        rows.append(jnp.sum(gradient[:, offset:] * signal[:, :-offset], axis=1))
    return jnp.stack(rows)


def reference(inputs, short_weights, filters, skip, grad_out):
    blocks = CHANNELS // FILTERS
    padded = 2 * SEQ
    spec_filter = jnp.fft.rfft(filters, n=padded, axis=1)
    branch_blocks = jnp.swapaxes(inputs.reshape(3, blocks, FILTERS, SEQ), 0, 1)
    tap_blocks = jnp.transpose(short_weights.reshape(3, KS, blocks, FILTERS), (2, 0, 1, 3))
    skip_blocks = skip.reshape(blocks, FILTERS)
    grad_blocks = grad_out.reshape(blocks, FILTERS, SEQ)

    def one_block(items):
        branches, taps, direct, cotangent = items
        signals = branches.astype(jnp.float32)
        grad = cotangent.astype(jnp.float32)
        query = causal_short(signals[0], taps[0])
        key_part = causal_short(signals[1], taps[1])
        value = causal_short(signals[2], taps[2])
        product = key_part * value
        spec_product = jnp.fft.rfft(product, n=padded, axis=1)
        conv_out = jnp.fft.irfft(spec_filter * spec_product, n=padded, axis=1)[:, :SEQ]
        conv_out = conv_out + direct[:, None] * product
        dw = grad * query
        spec_dw = jnp.fft.rfft(dw, n=padded, axis=1)
        dz = jnp.fft.irfft(spec_dw * jnp.conj(spec_filter), n=padded, axis=1)[:, :SEQ]
        dz = dz + direct[:, None] * dw
        filter_part = jnp.fft.irfft(spec_dw * jnp.conj(spec_product), n=padded, axis=1)[:, :SEQ]
        skip_part = jnp.sum(dw * product, axis=1)
        grads = [grad * conv_out, dz * value, dz * key_part]
        in_grads = jnp.stack([adjoint_short(grads[b], taps[b]) for b in range(3)])
        short_part = jnp.stack([short_terms(grads[b], signals[b]) for b in range(3)])
        return in_grads, filter_part, skip_part, short_part

    in_grads, filter_parts, skip_parts, short_parts = lax.map(one_block, (branch_blocks, tap_blocks, skip_blocks, grad_blocks))
    scale = SEQ ** -0.5
    input_grads = jnp.swapaxes(in_grads, 0, 1).reshape(3, CHANNELS, SEQ)
    filter_grad = jnp.sum(filter_parts, axis=0) * ((SEQ * blocks) ** -0.5)
    skip_grad = skip_parts.reshape(CHANNELS) * scale
    short_grad = jnp.transpose(short_parts, (1, 2, 0, 3)).reshape(3, KS, CHANNELS) * scale
    return input_grads, filter_grad, skip_grad, short_grad
```

```python
import math

import jax
import jax.numpy as jnp
import numpy as np
from jax import lax
from jax.experimental import pallas as pl
from jax.experimental.pallas import tpu as pltpu
from jax.sharding import PartitionSpec as P

f32 = jnp.float32
bf16 = jnp.bfloat16
BLOCKS = 64
SPAN = 256
HALF = 128
FILTERS = 32
GROUPS = 8
TAPS = 3
TOTAL = BLOCKS * SPAN


def split_table(values):
    high = values.astype(jnp.bfloat16)
    low = (values - high.astype(np.float64)).astype(jnp.bfloat16)
    return high, low


def tables():
    rows = np.arange(BLOCKS)
    cols = np.arange(SPAN)
    odd = 4 * rows + 1
    outer = 2 * math.pi * (odd[:, None] * rows[None, :] % 256) / 256.0
    g = np.concatenate([np.cos(outer), -np.sin(outer)], axis=0)
    g_high, g_low = split_table(g)
    forward_rows = np.concatenate([g_high, g_high, g_low], axis=1)
    t = g.T / TOTAL
    t_high, t_low = split_table(t)
    inverse_rows = np.concatenate([t_high, t_high, t_low], axis=1)
    inner = 2 * math.pi * (cols[:, None] * cols[None, :] % SPAN) / SPAN
    f = np.concatenate([np.cos(inner), np.sin(inner)], axis=1)
    f_high, f_low = split_table(f)
    turn = 2 * math.pi * (odd[:, None] * cols[None, :]) / (4.0 * TOTAL)
    turn = np.stack([np.cos(turn), np.sin(turn)]).astype(np.float32)
    return forward_rows, inverse_rows, f_high, f_low, turn


def halves(x):
    high = x.astype(bf16)
    return high, (x - high.astype(f32)).astype(bf16)


def dot(a, b):
    return jnp.dot(a, b, preferred_element_type=f32)


def dot_left(table, x):
    high, low = halves(x)
    return dot(table, jnp.concatenate([high, low, high], axis=0))


def dot_right(x, f_high, f_low):
    high, low = halves(x)
    return dot(high, f_high) + dot(low, f_high) + dot(high, f_low)


def later(x, n):
    row = lax.broadcasted_iota(jnp.int32, x.shape, 0)
    col = lax.broadcasted_iota(jnp.int32, x.shape, 1)
    here = pltpu.roll(x, n, 1)
    above = jnp.where(row == 0, 0.0, pltpu.roll(here, 1, 0))
    return jnp.where(col < n, above, here)


def sooner(x, n):
    row = lax.broadcasted_iota(jnp.int32, x.shape, 0)
    col = lax.broadcasted_iota(jnp.int32, x.shape, 1)
    here = pltpu.roll(x, SPAN - n, 1)
    below = jnp.where(row == BLOCKS - 1, 0.0, pltpu.roll(here, BLOCKS - 1, 0))
    return jnp.where(col >= SPAN - n, below, here)


def pack_kernel(inputs_ref, grad_ref, filters_ref, out_ref, rows_ref):
    h = filters_ref[...]
    h_high = h.astype(bf16).astype(f32)
    parts = [inputs_ref[b].astype(f32) for b in range(3)]
    parts += [grad_ref[...].astype(f32), h_high, h - h_high]
    rows_ref[...] = jnp.zeros_like(rows_ref)
    for i, part in enumerate(parts):
        for side in range(2):
            piece = part[:, side * HALF : (side + 1) * HALF]
            for copy in range(2):
                rows_ref[pl.ds(16 * copy + 2 * i + side, FILTERS, stride=32), :] = piece
    out_ref[...] = rows_ref[...].reshape(BLOCKS, 16, HALF).astype(bf16)


def spread(values, lanes):
    out = jnp.zeros((BLOCKS, HALF), f32)
    for i, value in enumerate(values):
        out = jnp.where(lanes == i, value, out)
    return out


def whole_sum(x):
    return jnp.sum(jnp.sum(x, axis=0, keepdims=True), axis=1, keepdims=True)


def channel_kernel(
    data_ref, taps_ref, skip_ref, left_ref, right_ref, f_high_ref, f_low_ref, turn_ref, out_ref, rows_ref
):
    place = lax.axis_index("seq")
    channel = place // 2
    rows_ref[...] = data_ref[...].astype(f32).reshape(BLOCKS * 16, HALF)

    def part(i):
        return jnp.concatenate(
            [rows_ref[pl.ds(2 * i + side, BLOCKS, stride=16), :] for side in range(2)], axis=1
        )

    branch = [part(b) for b in range(3)]
    grad = part(3)
    h_high, h_low = part(4), part(5)
    taps = [[taps_ref[b, j, channel] for j in range(TAPS)] for b in range(3)]
    direct = skip_ref[channel]
    moved = [[branch[b]] + [later(branch[b], j) for j in range(1, TAPS)] for b in range(3)]
    query, key, value = [
        taps[b][0] * moved[b][0] + taps[b][1] * moved[b][1] + taps[b][2] * moved[b][2]
        for b in range(3)
    ]
    product = key * value
    dw = grad * query

    cosine, sine = turn_ref[0], turn_ref[1]
    f_high, f_low = f_high_ref[...], f_low_ref[...]
    start = dot_left(left_ref[...], jnp.concatenate([product, dw, h_high + h_low], axis=1))
    stacked = []
    for i in range(3):
        re = start[:BLOCKS, i * SPAN : (i + 1) * SPAN]
        im = start[BLOCKS:, i * SPAN : (i + 1) * SPAN]
        stacked.append(re * cosine + im * sine)
        stacked.append(im * cosine - re * sine)
    spec = dot_right(jnp.concatenate(stacked, axis=0), f_high, f_low)

    def spectrum(i):
        re = spec[2 * i * BLOCKS : (2 * i + 1) * BLOCKS]
        im = spec[(2 * i + 1) * BLOCKS : (2 * i + 2) * BLOCKS]
        return re[:, :SPAN] + im[:, SPAN:], im[:, :SPAN] - re[:, SPAN:]

    (p_re, p_im), (d_re, d_im), (h_re, h_im) = [spectrum(i) for i in range(3)]
    joined = jnp.concatenate(
        [
            h_re * p_re - h_im * p_im,
            h_re * p_im + h_im * p_re,
            d_re * h_re + d_im * h_im,
            d_im * h_re - d_re * h_im,
            d_re * p_re + d_im * p_im,
            d_im * p_re - d_re * p_im,
        ],
        axis=0,
    )
    back = dot_right(joined, f_high, f_low)
    turned = []
    for i in range(3):
        re = back[2 * i * BLOCKS : (2 * i + 1) * BLOCKS]
        im = back[(2 * i + 1) * BLOCKS : (2 * i + 2) * BLOCKS]
        b_re = re[:, :SPAN] - im[:, SPAN:]
        b_im = im[:, :SPAN] + re[:, SPAN:]
        turned.append(
            jnp.concatenate([b_re * cosine - b_im * sine, b_im * cosine + b_re * sine], axis=0)
        )
    result = dot_left(right_ref[...], jnp.concatenate(turned, axis=1))
    conv_out = result[:, :SPAN] + direct * product
    dz = result[:, SPAN : 2 * SPAN] + direct * dw
    corr = result[:, 2 * SPAN :]

    grads = [grad * conv_out, dz * value, dz * key]
    side = lax.rem(place, 2)

    def mine(x):
        return jnp.where(side == 0, x[:, :HALF], x[:, HALF:])

    out_ref[...] = jnp.zeros_like(out_ref)
    for b in range(3):
        g = grads[b]
        total = taps[b][0] * g + taps[b][1] * sooner(g, 1) + taps[b][2] * sooner(g, 2)
        out_ref[pl.ds(b, BLOCKS, stride=8), :] = mine(total)
    out_ref[pl.ds(3, BLOCKS, stride=8), :] = mine(corr)
    sums = [whole_sum(grads[b] * moved[b][j]) for b in range(3) for j in range(TAPS)]
    sums.append(whole_sum(dw * product))
    lanes = lax.broadcasted_iota(jnp.int32, (BLOCKS, HALF), 1)
    out_ref[pl.ds(4, BLOCKS, stride=8), :] = spread(sums, lanes) * TOTAL**-0.5


def filter_kernel(data_ref, out_ref):
    out_ref[...] = data_ref[pl.ds(3, BLOCKS, stride=8), :].reshape(GROUPS, 8, HALF)


def place_kernel(data_ref, grads_ref, skip_ref, short_ref):
    for b in range(3):
        for side in range(2):
            grads_ref[b, :, side * HALF : (side + 1) * HALF] = data_ref[
                pl.ds(8 * side + b, FILTERS, stride=16), :
            ]
    sums = data_ref[pl.ds(4, FILTERS, stride=16), :]
    padded = jnp.concatenate([sums, jnp.zeros((HALF - FILTERS, HALF), f32)], axis=0)
    flipped = padded.T[:, :FILTERS]
    for b in range(3):
        short_ref[b] = flipped[TAPS * b : TAPS * (b + 1), :]
    skip_ref[...] = flipped[9:10, :]


def sum_kernel(data_ref, out_ref, rows_ref):
    total = data_ref[0]
    for i in range(1, GROUPS):
        total = total + data_ref[i]
    rows_ref[...] = total * (TOTAL * GROUPS) ** -0.5
    for side in range(2):
        out_ref[:, side * HALF : (side + 1) * HALF] = rows_ref[pl.ds(side, 4, stride=2), :]


vmem = pl.BlockSpec(memory_space=pltpu.VMEM)
smem = pl.BlockSpec(memory_space=pltpu.SMEM)
params = pltpu.CompilerParams(vmem_limit_bytes=32 * 1024 * 1024)


def like(shape, dtype=f32):
    return jax.ShapeDtypeStruct(shape, dtype)


def body(inputs, short_weights, filters, skip, grad_out):
    left, right, f_high, f_low, turn = [jnp.asarray(table) for table in tables()]
    message = pl.pallas_call(
        pack_kernel,
        out_shape=like((BLOCKS, 16, HALF), bf16),
        in_specs=[vmem] * 3,
        out_specs=vmem,
        scratch_shapes=[pltpu.VMEM((BLOCKS * 16, HALF), f32)],
        compiler_params=params,
    )(inputs, grad_out, filters)
    data = lax.all_to_all(message, "seq", split_axis=0, concat_axis=0, tiled=True)
    answer = pl.pallas_call(
        channel_kernel,
        out_shape=like((BLOCKS * 8, HALF)),
        in_specs=[vmem, smem, smem] + [vmem] * 5,
        out_specs=vmem,
        scratch_shapes=[pltpu.VMEM((BLOCKS * 16, HALF), f32)],
        compiler_params=params,
    )(data, short_weights, skip, left, right, f_high, f_low, turn)
    answer = lax.all_to_all(
        answer.reshape(BLOCKS, 8, HALF), "seq", split_axis=0, concat_axis=0, tiled=True
    ).reshape(BLOCKS * 8, HALF)
    partial = pl.pallas_call(
        filter_kernel,
        out_shape=like((GROUPS, 8, HALF)),
        in_specs=[vmem],
        out_specs=vmem,
        compiler_params=params,
    )(answer)
    partial = lax.all_to_all(partial, "chan", split_axis=0, concat_axis=0, tiled=True)
    grads, skip_grad, short_grad = pl.pallas_call(
        place_kernel,
        out_shape=(like((3, FILTERS, SPAN)), like((1, FILTERS)), like((3, TAPS, FILTERS))),
        in_specs=[vmem],
        out_specs=(vmem,) * 3,
        compiler_params=params,
    )(answer)
    filter_grad = pl.pallas_call(
        sum_kernel,
        out_shape=like((4, SPAN)),
        in_specs=[vmem],
        out_specs=vmem,
        scratch_shapes=[pltpu.VMEM((8, HALF), f32)],
        compiler_params=params,
    )(partial)
    return grads, filter_grad, skip_grad.reshape(FILTERS), short_grad


def solution(mesh):
    placed = (
        P(None, "chan", "seq"),
        P(None, None, "chan"),
        P(None, "seq"),
        P("chan"),
        P("chan", "seq"),
    )
    return jax.shard_map(
        body,
        mesh=mesh,
        in_specs=placed,
        out_specs=(P(None, "chan", "seq"), P("chan", "seq"), P("chan"), P(None, None, "chan")),
        check_vma=False,
    )
```

```python
import math

import jax
import jax.numpy as jnp
import numpy as np
from jax import lax
from jax.experimental import pallas as pl
from jax.experimental.pallas import tpu as pltpu
from jax.sharding import PartitionSpec as P

f32 = jnp.float32
bf16 = jnp.bfloat16
BLOCKS = 64
SPAN = 256
HALF = 128
FILTERS = 32
GROUPS = 8
TAPS = 3
ROWS = 5
TOTAL = BLOCKS * SPAN


def split_table(values):
    high = values.astype(jnp.bfloat16)
    low = (values - high.astype(np.float64)).astype(jnp.bfloat16)
    return high, low


def tables():
    rows = np.arange(BLOCKS)
    cols = np.arange(SPAN)
    odd = 4 * rows + 1
    outer = 2 * math.pi * (odd[:, None] * rows[None, :] % 256) / 256.0
    g = np.concatenate([np.cos(outer), -np.sin(outer)], axis=0)
    g_high, g_low = split_table(g)
    forward_rows = np.concatenate([g_high, g_high, g_low], axis=1)
    t = g.T / TOTAL
    t_high, t_low = split_table(t)
    inverse_rows = np.concatenate([t_high, t_high, t_low], axis=1)
    inner = 2 * math.pi * (cols[:, None] * cols[None, :] % SPAN) / SPAN
    f = np.concatenate([np.cos(inner), np.sin(inner)], axis=1)
    f_high, f_low = split_table(f)
    turn = 2 * math.pi * (odd[:, None] * cols[None, :]) / (4.0 * TOTAL)
    turn = np.stack([np.cos(turn), np.sin(turn)]).astype(np.float32)
    return forward_rows, inverse_rows, f_high, f_low, turn


def halves(x):
    high = x.astype(bf16)
    return high, (x - high.astype(f32)).astype(bf16)


def place_of(i):
    return i % 4, slice(i // 4 * HALF, (i // 4 + 1) * HALF)


def dot(a, b):
    return jnp.dot(a, b, preferred_element_type=f32)


def dot_left(table, x):
    high, low = halves(x)
    return dot(table, jnp.concatenate([high, low, high], axis=0))


def dot_right(x, f_high, f_low):
    high, low = halves(x)
    return dot(high, f_high) + dot(low, f_high) + dot(high, f_low)


def later(x, n):
    row = lax.broadcasted_iota(jnp.int32, x.shape, 0)
    col = lax.broadcasted_iota(jnp.int32, x.shape, 1)
    here = pltpu.roll(x, n, 1)
    above = jnp.where(row == 0, 0.0, pltpu.roll(here, 1, 0))
    return jnp.where(col < n, above, here)


def sooner(x, n):
    row = lax.broadcasted_iota(jnp.int32, x.shape, 0)
    col = lax.broadcasted_iota(jnp.int32, x.shape, 1)
    here = pltpu.roll(x, SPAN - n, 1)
    below = jnp.where(row == BLOCKS - 1, 0.0, pltpu.roll(here, BLOCKS - 1, 0))
    return jnp.where(col >= SPAN - n, below, here)


def pack_kernel(inputs_hbm, grad_hbm, filters_hbm, out_ref, inputs_ref, grad_ref, filters_ref, rows_ref, sems):
    copies = [
        pltpu.make_async_copy(source, target, sems.at[i])
        for i, (source, target) in enumerate(
            [(inputs_hbm, inputs_ref), (grad_hbm, grad_ref), (filters_hbm, filters_ref)]
        )
    ]
    for copy in copies:
        copy.start()
    for copy in copies:
        copy.wait()
    h = filters_ref[...]
    h_high = h.astype(bf16).astype(f32)
    parts = [inputs_ref[b].astype(f32) for b in range(3)]
    parts += [grad_ref[...].astype(f32), h_high, h - h_high]
    for i, part in enumerate(parts):
        for side in range(2):
            piece = part[:, side * HALF : (side + 1) * HALF]
            row, tile = place_of(2 * i + side)
            for copy in range(2):
                rows_ref[copy * FILTERS : (copy + 1) * FILTERS, row, tile] = piece
    out_ref[...] = rows_ref[...].astype(bf16)


def whole_sum(x):
    return jnp.sum(jnp.sum(x, axis=0, keepdims=True), axis=1, keepdims=True)


def channel_kernel(
    data_ref, taps_ref, skip_ref, left_ref, right_ref, f_high_ref, f_low_ref, turn_ref, out_ref, rows_ref
):
    place = lax.axis_index("seq")
    channel = lax.rem(place, FILTERS)
    rows_ref[...] = data_ref[...].astype(f32)

    def part(i):
        pieces = []
        for side in range(2):
            row, tile = place_of(2 * i + side)
            pieces.append(rows_ref[:, row, tile])
        return jnp.concatenate(pieces, axis=1)

    branch = [part(b) for b in range(3)]
    grad = part(3)
    h_high, h_low = part(4), part(5)
    taps = [[taps_ref[b, j, channel] for j in range(TAPS)] for b in range(3)]
    direct = skip_ref[channel]
    moved = [[branch[b]] + [later(branch[b], j) for j in range(1, TAPS)] for b in range(3)]
    query, key, value = [
        taps[b][0] * moved[b][0] + taps[b][1] * moved[b][1] + taps[b][2] * moved[b][2]
        for b in range(3)
    ]
    product = key * value
    dw = grad * query

    cosine, sine = turn_ref[0], turn_ref[1]
    f_high, f_low = f_high_ref[...], f_low_ref[...]
    start = dot_left(left_ref[...], jnp.concatenate([product, dw, h_high + h_low], axis=1))
    stacked = []
    for i in range(3):
        re = start[:BLOCKS, i * SPAN : (i + 1) * SPAN]
        im = start[BLOCKS:, i * SPAN : (i + 1) * SPAN]
        stacked.append(re * cosine + im * sine)
        stacked.append(im * cosine - re * sine)
    spec = dot_right(jnp.concatenate(stacked, axis=0), f_high, f_low)

    def spectrum(i):
        re = spec[2 * i * BLOCKS : (2 * i + 1) * BLOCKS]
        im = spec[(2 * i + 1) * BLOCKS : (2 * i + 2) * BLOCKS]
        return re[:, :SPAN] + im[:, SPAN:], im[:, :SPAN] - re[:, SPAN:]

    (p_re, p_im), (d_re, d_im), (h_re, h_im) = [spectrum(i) for i in range(3)]
    joined = jnp.concatenate(
        [
            h_re * p_re - h_im * p_im,
            h_re * p_im + h_im * p_re,
            d_re * h_re + d_im * h_im,
            d_im * h_re - d_re * h_im,
            d_re * p_re + d_im * p_im,
            d_im * p_re - d_re * p_im,
        ],
        axis=0,
    )
    back = dot_right(joined, f_high, f_low)
    turned = []
    for i in range(3):
        re = back[2 * i * BLOCKS : (2 * i + 1) * BLOCKS]
        im = back[(2 * i + 1) * BLOCKS : (2 * i + 2) * BLOCKS]
        b_re = re[:, :SPAN] - im[:, SPAN:]
        b_im = im[:, :SPAN] + re[:, SPAN:]
        turned.append(
            jnp.concatenate([b_re * cosine - b_im * sine, b_im * cosine + b_re * sine], axis=0)
        )
    result = dot_left(right_ref[...], jnp.concatenate(turned, axis=1))
    conv_out = result[:, :SPAN] + direct * product
    dz = result[:, SPAN : 2 * SPAN] + direct * dw
    corr = result[:, 2 * SPAN :]

    grads = [grad * conv_out, dz * value, dz * key]
    side = place // FILTERS

    def mine(x):
        return jnp.where(side == 0, x[:, :HALF], x[:, HALF:])

    for b in range(3):
        g = grads[b]
        total = taps[b][0] * g + taps[b][1] * sooner(g, 1) + taps[b][2] * sooner(g, 2)
        out_ref[pl.ds(b, BLOCKS, stride=ROWS), :] = mine(total)
    out_ref[pl.ds(3, BLOCKS, stride=ROWS), :] = mine(corr)
    sums = [whole_sum(grads[b] * moved[b][j]) for b in range(3) for j in range(TAPS)]
    sums.append(whole_sum(dw * product))
    lanes = lax.broadcasted_iota(jnp.int32, (1, HALF), 1)
    line = jnp.zeros((1, HALF), f32)
    for i, value in enumerate(sums):
        line = jnp.where(lanes == i, value, line)
    out_ref[pl.ds(4, BLOCKS, stride=ROWS), :] = jnp.broadcast_to(line * TOTAL**-0.5, (BLOCKS, HALF))


def filter_kernel(data_ref, out_ref):
    for group in range(GROUPS):
        for side in range(2):
            first = ROWS * (FILTERS * side + 4 * group) + 3
            out_ref[group, 4 * side : 4 * side + 4, :] = data_ref[pl.ds(first, 4, stride=ROWS), :]


def place_kernel(data_ref, partial_ref, grads_ref, skip_ref, short_ref, filter_ref):
    for b in range(3):
        for side in range(2):
            grads_ref[b, :, side * HALF : (side + 1) * HALF] = data_ref[
                pl.ds(ROWS * FILTERS * side + b, FILTERS, stride=ROWS), :
            ]
    sums = data_ref[pl.ds(4, FILTERS, stride=ROWS), :]
    padded = jnp.concatenate([sums, jnp.zeros((HALF - FILTERS, HALF), f32)], axis=0)
    flipped = padded.T[:, :FILTERS]
    for b in range(3):
        short_ref[b] = flipped[TAPS * b : TAPS * (b + 1), :]
    skip_ref[...] = flipped[9:10, :]
    total = partial_ref[0]
    for i in range(1, GROUPS):
        total = total + partial_ref[i]
    total = total * (TOTAL * GROUPS) ** -0.5
    for side in range(2):
        filter_ref[:, side * HALF : (side + 1) * HALF] = total[4 * side : 4 * side + 4, :]


vmem = pl.BlockSpec(memory_space=pltpu.VMEM)
hbm = pl.BlockSpec(memory_space=pltpu.HBM)
smem = pl.BlockSpec(memory_space=pltpu.SMEM)
params = pltpu.CompilerParams(vmem_limit_bytes=32 * 1024 * 1024)
pack_params = pltpu.CompilerParams(vmem_limit_bytes=56 * 1024 * 1024)


def like(shape, dtype=f32):
    return jax.ShapeDtypeStruct(shape, dtype)


def body(inputs, short_weights, filters, skip, grad_out):
    left, right, f_high, f_low, turn = [jnp.asarray(table) for table in tables()]
    message = pl.pallas_call(
        pack_kernel,
        out_shape=like((BLOCKS, 4, 3 * HALF), bf16),
        in_specs=[hbm] * 3,
        out_specs=vmem,
        scratch_shapes=[
            pltpu.VMEM((3, FILTERS, SPAN), bf16),
            pltpu.VMEM((FILTERS, SPAN), bf16),
            pltpu.VMEM((FILTERS, SPAN), f32),
            pltpu.VMEM((BLOCKS, 4, 3 * HALF), f32),
            pltpu.SemaphoreType.DMA((3,)),
        ],
        compiler_params=pack_params,
    )(inputs, grad_out, filters)
    data = lax.all_to_all(message, "seq", split_axis=0, concat_axis=0, tiled=True)
    answer = pl.pallas_call(
        channel_kernel,
        out_shape=like((BLOCKS * ROWS, HALF)),
        in_specs=[vmem, smem, smem] + [vmem] * 5,
        out_specs=vmem,
        scratch_shapes=[pltpu.VMEM((BLOCKS, 4, 3 * HALF), f32)],
        compiler_params=params,
    )(data, short_weights, skip, left, right, f_high, f_low, turn)
    answer = lax.all_to_all(
        answer.reshape(BLOCKS, 1, ROWS * HALF), "seq", split_axis=0, concat_axis=0, tiled=True
    ).reshape(BLOCKS * ROWS, HALF)
    partial = pl.pallas_call(
        filter_kernel,
        out_shape=like((GROUPS, 8, HALF)),
        in_specs=[vmem],
        out_specs=vmem,
        compiler_params=params,
    )(answer)
    partial = lax.all_to_all(partial, "chan", split_axis=0, concat_axis=0, tiled=True)
    grads, skip_grad, short_grad, filter_grad = pl.pallas_call(
        place_kernel,
        out_shape=(
            like((3, FILTERS, SPAN)),
            like((1, FILTERS)),
            like((3, TAPS, FILTERS)),
            like((4, SPAN)),
        ),
        in_specs=[vmem] * 2,
        out_specs=(vmem,) * 4,
        compiler_params=params,
    )(answer, partial)
    return grads, filter_grad, skip_grad.reshape(FILTERS), short_grad


def solution(mesh):
    placed = (
        P(None, "chan", "seq"),
        P(None, None, "chan"),
        P(None, "seq"),
        P("chan"),
        P("chan", "seq"),
    )
    return jax.shard_map(
        body,
        mesh=mesh,
        in_specs=placed,
        out_specs=(P(None, "chan", "seq"), P("chan", "seq"), P("chan"), P(None, None, "chan")),
        check_vma=False,
    )
```

```python
import math

import jax
import jax.numpy as jnp
import numpy as np
from jax import lax
from jax.experimental import pallas as pl
from jax.experimental.pallas import tpu as pltpu
from jax.sharding import PartitionSpec as P

f32 = jnp.float32
bf16 = jnp.bfloat16
BLOCKS = 64
SPAN = 256
HALF = 128
FILTERS = 32
GROUPS = 8
TAPS = 3
ROWS = 5
TOTAL = BLOCKS * SPAN


def split_table(values):
    high = values.astype(jnp.bfloat16)
    low = (values - high.astype(np.float64)).astype(jnp.bfloat16)
    return high, low


def tables():
    rows = np.arange(BLOCKS)
    cols = np.arange(SPAN)
    odd = 4 * rows + 1
    outer = 2 * math.pi * (odd[:, None] * rows[None, :] % 256) / 256.0
    g = np.concatenate([np.cos(outer), -np.sin(outer)], axis=0)
    g_high, g_low = split_table(g)
    forward_rows = np.concatenate([g_high, g_high, g_low], axis=1)
    t = g.T / TOTAL
    t_high, t_low = split_table(t)
    inverse_rows = np.concatenate([t_high, t_low], axis=1)
    inner = 2 * math.pi * (cols[:, None] * cols[None, :] % SPAN) / SPAN
    f = np.concatenate([np.cos(inner), np.sin(inner)], axis=1)
    f_high, f_low = split_table(f)
    strip = np.zeros((3 * BLOCKS, SPAN), dtype=jnp.bfloat16)
    strip[: 2 * BLOCKS, : 3 * BLOCKS] = forward_rows
    strip[2 * BLOCKS :] = inverse_rows
    eight = np.arange(8)
    coarse = 2 * math.pi * (32 * eight[:, None] * cols[None, :]) / (4.0 * TOTAL)
    fine = 2 * math.pi * ((4 * eight + 1)[:, None] * cols[None, :]) / (4.0 * TOTAL)
    turn = np.concatenate([np.cos(coarse), np.sin(coarse), np.cos(fine), np.sin(fine)])
    turn = turn.astype(np.float32)
    return f_high, f_low, strip, turn


def halves(x):
    high = x.astype(bf16)
    return high, (x - high.astype(f32)).astype(bf16)


def place_of(i):
    return i % 4, slice(i // 4 * HALF, (i // 4 + 1) * HALF)


def dot(a, b):
    return jnp.dot(a, b, preferred_element_type=f32)


def dot_left(table, x):
    high, low = halves(x)
    return dot(table, jnp.concatenate([high, low, high], axis=0))


def dot_right(x, f_high, f_low):
    high, low = halves(x)
    return dot(high, f_high) + dot(low, f_high) + dot(high, f_low)


def later(x, n):
    row = lax.broadcasted_iota(jnp.int32, x.shape, 0)
    col = lax.broadcasted_iota(jnp.int32, x.shape, 1)
    here = pltpu.roll(x, n, 1)
    above = jnp.where(row == 0, 0.0, pltpu.roll(here, 1, 0))
    return jnp.where(col < n, above, here)


def sooner(x, n):
    row = lax.broadcasted_iota(jnp.int32, x.shape, 0)
    col = lax.broadcasted_iota(jnp.int32, x.shape, 1)
    here = pltpu.roll(x, SPAN - n, 1)
    below = jnp.where(row == BLOCKS - 1, 0.0, pltpu.roll(here, BLOCKS - 1, 0))
    return jnp.where(col >= SPAN - n, below, here)


def pack_kernel(inputs_hbm, grad_hbm, filters_hbm, out_ref, inputs_ref, grad_ref, filters_ref, rows_ref, sems):
    copies = [
        pltpu.make_async_copy(source, target, sems.at[i])
        for i, (source, target) in enumerate(
            [(inputs_hbm, inputs_ref), (grad_hbm, grad_ref), (filters_hbm, filters_ref)]
        )
    ]
    for copy in copies:
        copy.start()
    for copy in copies:
        copy.wait()
    h = filters_ref[...]
    h_high = h.astype(bf16).astype(f32)
    parts = [inputs_ref[b].astype(f32) for b in range(3)]
    parts += [grad_ref[...].astype(f32), h_high, h - h_high]
    for i, part in enumerate(parts):
        for side in range(2):
            piece = part[:, side * HALF : (side + 1) * HALF]
            row, tile = place_of(2 * i + side)
            for copy in range(2):
                rows_ref[copy * FILTERS : (copy + 1) * FILTERS, row, tile] = piece
    out_ref[...] = rows_ref[...].astype(bf16)


def whole_sum(x):
    return jnp.sum(jnp.sum(x, axis=0, keepdims=True), axis=1, keepdims=True)


def turns(turn_ref):
    cosines, sines = [], []
    fine_cos, fine_sin = turn_ref[16:24, :], turn_ref[24:32, :]
    for a in range(8):
        coarse_cos, coarse_sin = turn_ref[a : a + 1, :], turn_ref[8 + a : 9 + a, :]
        cosines.append(coarse_cos * fine_cos - coarse_sin * fine_sin)
        sines.append(coarse_sin * fine_cos + coarse_cos * fine_sin)
    return jnp.concatenate(cosines, axis=0), jnp.concatenate(sines, axis=0)


def channel_kernel(
    data_ref, taps_ref, skip_ref, high_ref, low_ref, strip_ref, turn_ref, out_ref, rows_ref
):
    place = lax.axis_index("seq")
    channel = lax.rem(place, FILTERS)
    rows_ref[...] = data_ref[...].astype(f32)

    def part(i):
        pieces = []
        for side in range(2):
            row, tile = place_of(2 * i + side)
            pieces.append(rows_ref[:, row, tile])
        return jnp.concatenate(pieces, axis=1)

    branch = [part(b) for b in range(3)]
    grad = part(3)
    h_high, h_low = part(4), part(5)
    taps = [[taps_ref[b, j, channel] for j in range(TAPS)] for b in range(3)]
    direct = skip_ref[channel]
    moved = [[branch[b]] + [later(branch[b], j) for j in range(1, TAPS)] for b in range(3)]
    query, key, value = [
        taps[b][0] * moved[b][0] + taps[b][1] * moved[b][1] + taps[b][2] * moved[b][2]
        for b in range(3)
    ]
    product = key * value
    dw = grad * query

    cosine, sine = turns(turn_ref)
    f_high, f_low = high_ref[...], low_ref[...]
    left = strip_ref[: 2 * BLOCKS, : 3 * BLOCKS]
    right = strip_ref[2 * BLOCKS :, :]
    right = jnp.concatenate([right[:, :HALF], right], axis=1)
    start = dot_left(left, jnp.concatenate([product, dw, h_high + h_low], axis=1))
    stacked = []
    for i in range(3):
        re = start[:BLOCKS, i * SPAN : (i + 1) * SPAN]
        im = start[BLOCKS:, i * SPAN : (i + 1) * SPAN]
        stacked.append(re * cosine + im * sine)
        stacked.append(im * cosine - re * sine)
    spec = dot_right(jnp.concatenate(stacked, axis=0), f_high, f_low)

    def spectrum(i):
        re = spec[2 * i * BLOCKS : (2 * i + 1) * BLOCKS]
        im = spec[(2 * i + 1) * BLOCKS : (2 * i + 2) * BLOCKS]
        return re[:, :SPAN] + im[:, SPAN:], im[:, :SPAN] - re[:, SPAN:]

    (p_re, p_im), (d_re, d_im), (h_re, h_im) = [spectrum(i) for i in range(3)]
    joined = jnp.concatenate(
        [
            h_re * p_re - h_im * p_im,
            h_re * p_im + h_im * p_re,
            d_re * h_re + d_im * h_im,
            d_im * h_re - d_re * h_im,
            d_re * p_re + d_im * p_im,
            d_im * p_re - d_re * p_im,
        ],
        axis=0,
    )
    back = dot_right(joined, f_high, f_low)
    turned = []
    for i in range(3):
        re = back[2 * i * BLOCKS : (2 * i + 1) * BLOCKS]
        im = back[(2 * i + 1) * BLOCKS : (2 * i + 2) * BLOCKS]
        b_re = re[:, :SPAN] - im[:, SPAN:]
        b_im = im[:, :SPAN] + re[:, SPAN:]
        turned.append(
            jnp.concatenate([b_re * cosine - b_im * sine, b_im * cosine + b_re * sine], axis=0)
        )
    result = dot_left(right, jnp.concatenate(turned, axis=1))
    conv_out = result[:, :SPAN] + direct * product
    dz = result[:, SPAN : 2 * SPAN] + direct * dw
    corr = result[:, 2 * SPAN :]

    grads = [grad * conv_out, dz * value, dz * key]
    side = place // FILTERS

    def mine(x):
        return jnp.where(side == 0, x[:, :HALF], x[:, HALF:])

    for b in range(3):
        g = grads[b]
        total = taps[b][0] * g + taps[b][1] * sooner(g, 1) + taps[b][2] * sooner(g, 2)
        out_ref[pl.ds(b, BLOCKS, stride=ROWS), :] = mine(total)
    out_ref[pl.ds(3, BLOCKS, stride=ROWS), :] = mine(corr)
    sums = [whole_sum(grads[b] * moved[b][j]) for b in range(3) for j in range(TAPS)]
    sums.append(whole_sum(dw * product))
    lanes = lax.broadcasted_iota(jnp.int32, (1, HALF), 1)
    line = jnp.zeros((1, HALF), f32)
    for i, value in enumerate(sums):
        line = jnp.where(lanes == i, value, line)
    out_ref[pl.ds(4, BLOCKS, stride=ROWS), :] = jnp.broadcast_to(line * TOTAL**-0.5, (BLOCKS, HALF))


def filter_kernel(data_ref, out_ref):
    for group in range(GROUPS):
        for side in range(2):
            first = ROWS * (FILTERS * side + 4 * group) + 3
            out_ref[group, 4 * side : 4 * side + 4, :] = data_ref[pl.ds(first, 4, stride=ROWS), :]


def place_kernel(data_ref, partial_ref, grads_ref, skip_ref, short_ref, filter_ref):
    for b in range(3):
        for side in range(2):
            grads_ref[b, :, side * HALF : (side + 1) * HALF] = data_ref[
                pl.ds(ROWS * FILTERS * side + b, FILTERS, stride=ROWS), :
            ]
    sums = data_ref[pl.ds(4, FILTERS, stride=ROWS), :]
    padded = jnp.concatenate([sums, jnp.zeros((HALF - FILTERS, HALF), f32)], axis=0)
    flipped = padded.T[:, :FILTERS]
    for b in range(3):
        short_ref[b] = flipped[TAPS * b : TAPS * (b + 1), :]
    skip_ref[...] = flipped[9:10, :]
    total = partial_ref[0]
    for i in range(1, GROUPS):
        total = total + partial_ref[i]
    total = total * (TOTAL * GROUPS) ** -0.5
    for side in range(2):
        filter_ref[:, side * HALF : (side + 1) * HALF] = total[4 * side : 4 * side + 4, :]


vmem = pl.BlockSpec(memory_space=pltpu.VMEM)
hbm = pl.BlockSpec(memory_space=pltpu.HBM)
smem = pl.BlockSpec(memory_space=pltpu.SMEM)
params = pltpu.CompilerParams(vmem_limit_bytes=32 * 1024 * 1024)
pack_params = pltpu.CompilerParams(vmem_limit_bytes=56 * 1024 * 1024)


def like(shape, dtype=f32):
    return jax.ShapeDtypeStruct(shape, dtype)


def body(inputs, short_weights, filters, skip, grad_out):
    f_high, f_low, strip, turn = [jnp.asarray(values) for values in tables()]
    message = pl.pallas_call(
        pack_kernel,
        out_shape=like((BLOCKS, 4, 3 * HALF), bf16),
        in_specs=[hbm] * 3,
        out_specs=vmem,
        scratch_shapes=[
            pltpu.VMEM((3, FILTERS, SPAN), bf16),
            pltpu.VMEM((FILTERS, SPAN), bf16),
            pltpu.VMEM((FILTERS, SPAN), f32),
            pltpu.VMEM((BLOCKS, 4, 3 * HALF), f32),
            pltpu.SemaphoreType.DMA((3,)),
        ],
        compiler_params=pack_params,
    )(inputs, grad_out, filters)
    data = lax.all_to_all(message, "seq", split_axis=0, concat_axis=0, tiled=True)
    answer = pl.pallas_call(
        channel_kernel,
        out_shape=like((BLOCKS * ROWS, HALF)),
        in_specs=[vmem, smem, smem] + [vmem] * 4,
        out_specs=vmem,
        scratch_shapes=[pltpu.VMEM((BLOCKS, 4, 3 * HALF), f32)],
        compiler_params=params,
    )(data, short_weights, skip, f_high, f_low, strip, turn)
    answer = lax.all_to_all(
        answer.reshape(BLOCKS, 1, ROWS * HALF), "seq", split_axis=0, concat_axis=0, tiled=True
    ).reshape(BLOCKS * ROWS, HALF)
    partial = pl.pallas_call(
        filter_kernel,
        out_shape=like((GROUPS, 8, HALF)),
        in_specs=[vmem],
        out_specs=vmem,
        compiler_params=params,
    )(answer)
    partial = lax.all_to_all(partial, "chan", split_axis=0, concat_axis=0, tiled=True)
    grads, skip_grad, short_grad, filter_grad = pl.pallas_call(
        place_kernel,
        out_shape=(
            like((3, FILTERS, SPAN)),
            like((1, FILTERS)),
            like((3, TAPS, FILTERS)),
            like((4, SPAN)),
        ),
        in_specs=[vmem] * 2,
        out_specs=(vmem,) * 4,
        compiler_params=params,
    )(answer, partial)
    return grads, filter_grad, skip_grad.reshape(FILTERS), short_grad


def solution(mesh):
    placed = (
        P(None, "chan", "seq"),
        P(None, None, "chan"),
        P(None, "seq"),
        P("chan"),
        P("chan", "seq"),
    )
    return jax.shard_map(
        body,
        mesh=mesh,
        in_specs=placed,
        out_specs=(P(None, "chan", "seq"), P("chan", "seq"), P("chan"), P(None, None, "chan")),
        check_vma=False,
    )
```

```python
import math

import jax
import jax.numpy as jnp
import numpy as np
from jax import lax
from jax.experimental import pallas as pl
from jax.experimental.pallas import tpu as pltpu
from jax.sharding import PartitionSpec as P

f32 = jnp.float32
bf16 = jnp.bfloat16
BLOCKS = 64
SPAN = 256
HALF = 128
FILTERS = 32
GROUPS = 8
TAPS = 3
ROWS = 9
RUN = 8
PARTNERS = [[16 * a + RUN * b + z for a in range(4) for z in range(RUN)] for b in range(2)]
TOTAL = BLOCKS * SPAN


def split_table(values):
    high = values.astype(jnp.bfloat16)
    low = (values - high.astype(np.float64)).astype(jnp.bfloat16)
    return high, low


def tables():
    rows = np.arange(BLOCKS)
    cols = np.arange(SPAN)
    odd = 4 * rows + 1
    outer = 2 * math.pi * (odd[:, None] * rows[None, :] % 256) / 256.0
    g = np.concatenate([np.cos(outer), -np.sin(outer)], axis=0)
    g_high, g_low = split_table(g)
    forward_rows = np.concatenate([g_high, g_high, g_low], axis=1)
    t = g.T / TOTAL
    t_high, t_low = split_table(t)
    inverse_rows = np.concatenate([t_high, t_low], axis=1)
    inner = 2 * math.pi * (cols[:, None] * cols[None, :] % SPAN) / SPAN
    f = np.concatenate([np.cos(inner), np.sin(inner)], axis=1)
    f_high, f_low = split_table(f)
    strip = np.zeros((3 * BLOCKS, SPAN), dtype=jnp.bfloat16)
    strip[: 2 * BLOCKS, : 3 * BLOCKS] = forward_rows
    strip[2 * BLOCKS :] = inverse_rows
    eight = np.arange(8)
    coarse = 2 * math.pi * (32 * eight[:, None] * cols[None, :]) / (4.0 * TOTAL)
    fine = 2 * math.pi * ((4 * eight + 1)[:, None] * cols[None, :]) / (4.0 * TOTAL)
    turn = np.concatenate([np.cos(coarse), np.sin(coarse), np.cos(fine), np.sin(fine)])
    turn = turn.astype(np.float32)
    return f_high, f_low, strip, turn


def halves(x):
    high = x.astype(bf16)
    return high, (x - high.astype(f32)).astype(bf16)


def place_of(i):
    return i % 4, slice(i // 4 * HALF, (i // 4 + 1) * HALF)


def dot(a, b):
    return jnp.dot(a, b, preferred_element_type=f32)


def dot_left(table, x):
    high, low = halves(x)
    return dot(table, jnp.concatenate([high, low, high], axis=0))


def dot_right(x, f_high, f_low):
    high, low = halves(x)
    return dot(high, f_high) + dot(low, f_high) + dot(high, f_low)


def later(x, n):
    row = lax.broadcasted_iota(jnp.int32, x.shape, 0)
    col = lax.broadcasted_iota(jnp.int32, x.shape, 1)
    here = pltpu.roll(x, n, 1)
    above = jnp.where(row == 0, 0.0, pltpu.roll(here, 1, 0))
    return jnp.where(col < n, above, here)


def sooner(x, n):
    row = lax.broadcasted_iota(jnp.int32, x.shape, 0)
    col = lax.broadcasted_iota(jnp.int32, x.shape, 1)
    here = pltpu.roll(x, SPAN - n, 1)
    below = jnp.where(row == BLOCKS - 1, 0.0, pltpu.roll(here, BLOCKS - 1, 0))
    return jnp.where(col >= SPAN - n, below, here)


def pack_kernel(inputs_hbm, grad_hbm, filters_hbm, out_ref, inputs_ref, grad_ref, filters_ref, rows_ref, sems):
    copies = [
        pltpu.make_async_copy(source, target, sems.at[i])
        for i, (source, target) in enumerate(
            [(inputs_hbm, inputs_ref), (grad_hbm, grad_ref), (filters_hbm, filters_ref)]
        )
    ]
    for copy in copies:
        copy.start()
    for copy in copies:
        copy.wait()
    h = filters_ref[...]
    h_high = h.astype(bf16).astype(f32)
    parts = [inputs_ref[b].astype(f32) for b in range(3)]
    parts += [grad_ref[...].astype(f32), h_high, h - h_high]
    for i, part in enumerate(parts):
        for side in range(2):
            piece = part[:, side * HALF : (side + 1) * HALF]
            row, tile = place_of(2 * i + side)
            for first in range(0, BLOCKS, RUN):
                channel = first // (2 * RUN) * RUN
                rows_ref[first : first + RUN, row, tile] = piece[channel : channel + RUN]
    out_ref[...] = rows_ref[...].astype(bf16)


def whole_sum(x):
    return jnp.sum(jnp.sum(x, axis=0, keepdims=True), axis=1, keepdims=True)


def turns(turn_ref):
    cosines, sines = [], []
    fine_cos, fine_sin = turn_ref[16:24, :], turn_ref[24:32, :]
    for a in range(8):
        coarse_cos, coarse_sin = turn_ref[a : a + 1, :], turn_ref[8 + a : 9 + a, :]
        cosines.append(coarse_cos * fine_cos - coarse_sin * fine_sin)
        sines.append(coarse_sin * fine_cos + coarse_cos * fine_sin)
    return jnp.concatenate(cosines, axis=0), jnp.concatenate(sines, axis=0)


def channel_kernel(
    data_ref, taps_ref, skip_ref, high_ref, low_ref, strip_ref, turn_ref, out_ref, rows_ref
):
    place = lax.axis_index("seq")
    channel = place // (2 * RUN) * RUN + lax.rem(place, RUN)
    rows_ref[...] = data_ref[...].astype(f32)

    def part(i):
        pieces = []
        for side in range(2):
            row, tile = place_of(2 * i + side)
            pieces.append(rows_ref[:, row, tile])
        return jnp.concatenate(pieces, axis=1)

    branch = [part(b) for b in range(3)]
    grad = part(3)
    h_high, h_low = part(4), part(5)
    taps = [[taps_ref[b, j, channel] for j in range(TAPS)] for b in range(3)]
    direct = skip_ref[channel]
    moved = [[branch[b]] + [later(branch[b], j) for j in range(1, TAPS)] for b in range(3)]
    query, key, value = [
        taps[b][0] * moved[b][0] + taps[b][1] * moved[b][1] + taps[b][2] * moved[b][2]
        for b in range(3)
    ]
    product = key * value
    dw = grad * query

    cosine, sine = turns(turn_ref)
    f_high, f_low = high_ref[...], low_ref[...]
    left = strip_ref[: 2 * BLOCKS, : 3 * BLOCKS]
    right = strip_ref[2 * BLOCKS :, :]
    right = jnp.concatenate([right[:, :HALF], right], axis=1)
    start = dot_left(left, jnp.concatenate([product, dw, h_high + h_low], axis=1))
    stacked = []
    for i in range(3):
        re = start[:BLOCKS, i * SPAN : (i + 1) * SPAN]
        im = start[BLOCKS:, i * SPAN : (i + 1) * SPAN]
        stacked.append(re * cosine + im * sine)
        stacked.append(im * cosine - re * sine)
    spec = dot_right(jnp.concatenate(stacked, axis=0), f_high, f_low)

    def spectrum(i):
        re = spec[2 * i * BLOCKS : (2 * i + 1) * BLOCKS]
        im = spec[(2 * i + 1) * BLOCKS : (2 * i + 2) * BLOCKS]
        return re[:, :SPAN] + im[:, SPAN:], im[:, :SPAN] - re[:, SPAN:]

    (p_re, p_im), (d_re, d_im), (h_re, h_im) = [spectrum(i) for i in range(3)]
    joined = jnp.concatenate(
        [
            h_re * p_re - h_im * p_im,
            h_re * p_im + h_im * p_re,
            d_re * h_re + d_im * h_im,
            d_im * h_re - d_re * h_im,
            d_re * p_re + d_im * p_im,
            d_im * p_re - d_re * p_im,
        ],
        axis=0,
    )
    back = dot_right(joined, f_high, f_low)
    turned = []
    for i in range(3):
        re = back[2 * i * BLOCKS : (2 * i + 1) * BLOCKS]
        im = back[(2 * i + 1) * BLOCKS : (2 * i + 2) * BLOCKS]
        b_re = re[:, :SPAN] - im[:, SPAN:]
        b_im = im[:, :SPAN] + re[:, SPAN:]
        turned.append(
            jnp.concatenate([b_re * cosine - b_im * sine, b_im * cosine + b_re * sine], axis=0)
        )
    result = dot_left(right, jnp.concatenate(turned, axis=1))
    conv_out = result[:, :SPAN] + direct * product
    dz = result[:, SPAN : 2 * SPAN] + direct * dw
    corr = result[:, 2 * SPAN :]

    grads = [grad * conv_out, dz * value, dz * key]
    odd = lax.rem(place // RUN, 2)

    def give(x, row):
        runs = [
            jnp.where(odd == 0, x[first : first + RUN], x[first + RUN : first + 2 * RUN])
            for first in range(0, BLOCKS, 2 * RUN)
        ]
        mine = jnp.concatenate(runs, axis=0)
        for side in range(2):
            out_ref[pl.ds(row + side, FILTERS, stride=ROWS), :] = mine[
                :, side * HALF : (side + 1) * HALF
            ]

    for b in range(3):
        g = grads[b]
        give(taps[b][0] * g + taps[b][1] * sooner(g, 1) + taps[b][2] * sooner(g, 2), 2 * b)
    give(corr, 6)
    sums = [whole_sum(grads[b] * moved[b][j]) for b in range(3) for j in range(TAPS)]
    sums.append(whole_sum(dw * product))
    lanes = lax.broadcasted_iota(jnp.int32, (1, HALF), 1)
    line = jnp.zeros((1, HALF), f32)
    for i, value in enumerate(sums):
        line = jnp.where(lanes == i, value, line)
    line = jnp.broadcast_to(line * TOTAL**-0.5, (FILTERS, HALF))
    out_ref[pl.ds(8, FILTERS, stride=ROWS), :] = line


def filter_kernel(data_ref, out_ref):
    for group in range(GROUPS):
        for side in range(2):
            first = ROWS * 4 * group + 6 + side
            out_ref[group, 4 * side : 4 * side + 4, :] = data_ref[pl.ds(first, 4, stride=ROWS), :]


def place_kernel(data_ref, partial_ref, grads_ref, skip_ref, short_ref, filter_ref):
    for b in range(3):
        for side in range(2):
            grads_ref[b, :, side * HALF : (side + 1) * HALF] = data_ref[
                pl.ds(2 * b + side, FILTERS, stride=ROWS), :
            ]
    sums = data_ref[pl.ds(8, FILTERS, stride=ROWS), :]
    padded = jnp.concatenate([sums, jnp.zeros((HALF - FILTERS, HALF), f32)], axis=0)
    flipped = padded.T[:, :FILTERS]
    for b in range(3):
        short_ref[b] = flipped[TAPS * b : TAPS * (b + 1), :]
    skip_ref[...] = flipped[9:10, :]
    total = partial_ref[0]
    for i in range(1, GROUPS):
        total = total + partial_ref[i]
    total = total * (TOTAL * GROUPS) ** -0.5
    for side in range(2):
        filter_ref[:, side * HALF : (side + 1) * HALF] = total[4 * side : 4 * side + 4, :]


vmem = pl.BlockSpec(memory_space=pltpu.VMEM)
hbm = pl.BlockSpec(memory_space=pltpu.HBM)
smem = pl.BlockSpec(memory_space=pltpu.SMEM)
params = pltpu.CompilerParams(vmem_limit_bytes=32 * 1024 * 1024)
pack_params = pltpu.CompilerParams(vmem_limit_bytes=56 * 1024 * 1024)


def like(shape, dtype=f32):
    return jax.ShapeDtypeStruct(shape, dtype)


def body(inputs, short_weights, filters, skip, grad_out):
    f_high, f_low, strip, turn = [jnp.asarray(values) for values in tables()]
    message = pl.pallas_call(
        pack_kernel,
        out_shape=like((BLOCKS, 4, 3 * HALF), bf16),
        in_specs=[hbm] * 3,
        out_specs=vmem,
        scratch_shapes=[
            pltpu.VMEM((3, FILTERS, SPAN), bf16),
            pltpu.VMEM((FILTERS, SPAN), bf16),
            pltpu.VMEM((FILTERS, SPAN), f32),
            pltpu.VMEM((BLOCKS, 4, 3 * HALF), f32),
            pltpu.SemaphoreType.DMA((3,)),
        ],
        compiler_params=pack_params,
    )(inputs, grad_out, filters)
    data = lax.all_to_all(message, "seq", split_axis=0, concat_axis=0, tiled=True)
    answer = pl.pallas_call(
        channel_kernel,
        out_shape=like((FILTERS * ROWS, HALF)),
        in_specs=[vmem, smem, smem] + [vmem] * 4,
        out_specs=vmem,
        scratch_shapes=[pltpu.VMEM((BLOCKS, 4, 3 * HALF), f32)],
        compiler_params=params,
    )(data, short_weights, skip, f_high, f_low, strip, turn)
    answer = lax.all_to_all(
        answer.reshape(FILTERS, 1, ROWS * HALF),
        "seq",
        split_axis=0,
        concat_axis=0,
        tiled=True,
        axis_index_groups=PARTNERS,
    ).reshape(FILTERS * ROWS, HALF)
    partial = pl.pallas_call(
        filter_kernel,
        out_shape=like((GROUPS, 8, HALF)),
        in_specs=[vmem],
        out_specs=vmem,
        compiler_params=params,
    )(answer)
    partial = lax.all_to_all(partial, "chan", split_axis=0, concat_axis=0, tiled=True)
    grads, skip_grad, short_grad, filter_grad = pl.pallas_call(
        place_kernel,
        out_shape=(
            like((3, FILTERS, SPAN)),
            like((1, FILTERS)),
            like((3, TAPS, FILTERS)),
            like((4, SPAN)),
        ),
        in_specs=[vmem] * 2,
        out_specs=(vmem,) * 4,
        compiler_params=params,
    )(answer, partial)
    return grads, filter_grad, skip_grad.reshape(FILTERS), short_grad


def solution(mesh):
    placed = (
        P(None, "chan", "seq"),
        P(None, None, "chan"),
        P(None, "seq"),
        P("chan"),
        P("chan", "seq"),
    )
    return jax.shard_map(
        body,
        mesh=mesh,
        in_specs=placed,
        out_specs=(P(None, "chan", "seq"), P("chan", "seq"), P("chan"), P(None, None, "chan")),
        check_vma=False,
    )
```

```python
import math

import jax
import jax.numpy as jnp
import numpy as np
from jax import lax
from jax.experimental import pallas as pl
from jax.experimental.pallas import tpu as pltpu
from jax.sharding import PartitionSpec as P

f32 = jnp.float32
bf16 = jnp.bfloat16
BLOCKS = 64
SPAN = 256
HALF = 128
FILTERS = 32
GROUPS = 8
TAPS = 3
ROWS = 9
RUN = 8
PARTNERS = [[16 * a + RUN * b + z for a in range(4) for z in range(RUN)] for b in range(2)]
TOTAL = BLOCKS * SPAN


def split_table(values):
    high = values.astype(jnp.bfloat16)
    low = (values - high.astype(np.float64)).astype(jnp.bfloat16)
    return high, low


def tables():
    rows = np.arange(BLOCKS)
    cols = np.arange(SPAN)
    odd = 4 * rows + 1
    outer = 2 * math.pi * (odd[:, None] * rows[None, :] % 256) / 256.0
    g = np.concatenate([np.cos(outer), -np.sin(outer)], axis=0)
    g_high, g_low = split_table(g)
    forward_rows = np.concatenate([g_high, g_high, g_low], axis=1)
    t = g.T / TOTAL
    t_high, t_low = split_table(t)
    inverse_rows = np.concatenate([t_high, t_low], axis=1)
    near = np.arange(HALF)
    inner = 2 * math.pi * (near[:, None] * near[None, :] % HALF) / HALF
    f = np.concatenate([np.cos(inner), np.sin(inner)], axis=1)
    f_high, f_low = split_table(f)
    points = np.concatenate([f_high, f_high, f_low], axis=0)
    strip = np.zeros((3 * BLOCKS, SPAN), dtype=jnp.bfloat16)
    strip[: 2 * BLOCKS, : 3 * BLOCKS] = forward_rows
    strip[2 * BLOCKS :] = inverse_rows
    eight = np.arange(8)
    coarse = 2 * math.pi * (32 * eight[:, None] * cols[None, :]) / (4.0 * TOTAL)
    fine = 2 * math.pi * ((4 * eight + 1)[:, None] * cols[None, :]) / (4.0 * TOTAL)
    step = 2 * math.pi * near / SPAN
    step = np.concatenate([np.cos(step), np.sin(step)])[None, :] * np.ones((8, 1))
    turn = np.concatenate([np.cos(coarse), np.sin(coarse), np.cos(fine), np.sin(fine), step])
    turn = turn.astype(np.float32)
    return points, strip, turn


def halves(x):
    high = x.astype(bf16)
    return high, (x - high.astype(f32)).astype(bf16)


def place_of(i):
    return i % 4, slice(i // 4 * HALF, (i // 4 + 1) * HALF)


def dot(a, b):
    return jnp.dot(a, b, preferred_element_type=f32)


def dot_left(table, x):
    high, low = halves(x)
    return dot(table, jnp.concatenate([high, low, high], axis=0))


def dot_right(x, table):
    high, low = halves(x)
    return dot(jnp.concatenate([high, low, high], axis=1), table)


def later(x, n):
    row = lax.broadcasted_iota(jnp.int32, x.shape, 0)
    col = lax.broadcasted_iota(jnp.int32, x.shape, 1)
    here = pltpu.roll(x, n, 1)
    above = jnp.where(row == 0, 0.0, pltpu.roll(here, 1, 0))
    return jnp.where(col < n, above, here)


def sooner(x, n):
    row = lax.broadcasted_iota(jnp.int32, x.shape, 0)
    col = lax.broadcasted_iota(jnp.int32, x.shape, 1)
    here = pltpu.roll(x, SPAN - n, 1)
    below = jnp.where(row == BLOCKS - 1, 0.0, pltpu.roll(here, BLOCKS - 1, 0))
    return jnp.where(col >= SPAN - n, below, here)


def pack_kernel(inputs_hbm, grad_hbm, filters_hbm, out_ref, inputs_ref, grad_ref, filters_ref, rows_ref, sems):
    copies = [
        pltpu.make_async_copy(source, target, sems.at[i])
        for i, (source, target) in enumerate(
            [(inputs_hbm, inputs_ref), (grad_hbm, grad_ref), (filters_hbm, filters_ref)]
        )
    ]
    for copy in copies:
        copy.start()
    for copy in copies:
        copy.wait()
    h = filters_ref[...]
    h_high = h.astype(bf16).astype(f32)
    parts = [inputs_ref[b].astype(f32) for b in range(3)]
    parts += [grad_ref[...].astype(f32), h_high, h - h_high]
    for i, part in enumerate(parts):
        for side in range(2):
            piece = part[:, side * HALF : (side + 1) * HALF]
            row, tile = place_of(2 * i + side)
            for first in range(0, BLOCKS, RUN):
                channel = first // (2 * RUN) * RUN
                rows_ref[first : first + RUN, row, tile] = piece[channel : channel + RUN]
    out_ref[...] = rows_ref[...].astype(bf16)


def whole_sum(x):
    return jnp.sum(jnp.sum(x, axis=0, keepdims=True), axis=1, keepdims=True)


def turns(turn_ref):
    cosines, sines = [], []
    fine_cos, fine_sin = turn_ref[16:24, :], turn_ref[24:32, :]
    for a in range(8):
        coarse_cos, coarse_sin = turn_ref[a : a + 1, :], turn_ref[8 + a : 9 + a, :]
        cosines.append(coarse_cos * fine_cos - coarse_sin * fine_sin)
        sines.append(coarse_sin * fine_cos + coarse_cos * fine_sin)
    return jnp.concatenate(cosines, axis=0), jnp.concatenate(sines, axis=0)


def channel_kernel(
    data_ref, taps_ref, skip_ref, points_ref, strip_ref, turn_ref, out_ref, rows_ref
):
    place = lax.axis_index("seq")
    channel = place // (2 * RUN) * RUN + lax.rem(place, RUN)
    rows_ref[...] = data_ref[...].astype(f32)

    def part(i):
        pieces = []
        for side in range(2):
            row, tile = place_of(2 * i + side)
            pieces.append(rows_ref[:, row, tile])
        return jnp.concatenate(pieces, axis=1)

    branch = [part(b) for b in range(3)]
    grad = part(3)
    h_high, h_low = part(4), part(5)
    taps = [[taps_ref[b, j, channel] for j in range(TAPS)] for b in range(3)]
    direct = skip_ref[channel]
    moved = [[branch[b]] + [later(branch[b], j) for j in range(1, TAPS)] for b in range(3)]
    query, key, value = [
        taps[b][0] * moved[b][0] + taps[b][1] * moved[b][1] + taps[b][2] * moved[b][2]
        for b in range(3)
    ]
    product = key * value
    dw = grad * query

    cosine, sine = turns(turn_ref)
    points = points_ref[...]
    odd_cos, odd_sin = turn_ref[32:33, :HALF], turn_ref[32:33, HALF:]
    left = strip_ref[: 2 * BLOCKS, : 3 * BLOCKS]
    right = strip_ref[2 * BLOCKS :, :]
    right = jnp.concatenate([right[:, :HALF], right], axis=1)
    start = dot_left(left, jnp.concatenate([product, dw, h_high + h_low], axis=1))
    stacked = []
    for i in range(3):
        re = start[:BLOCKS, i * SPAN : (i + 1) * SPAN]
        im = start[BLOCKS:, i * SPAN : (i + 1) * SPAN]
        re, im = re * cosine + im * sine, im * cosine - re * sine
        stacked += [re[:, :HALF] + re[:, HALF:], im[:, :HALF] + im[:, HALF:]]
        re, im = re[:, :HALF] - re[:, HALF:], im[:, :HALF] - im[:, HALF:]
        stacked += [re * odd_cos + im * odd_sin, im * odd_cos - re * odd_sin]
    spec = dot_right(jnp.concatenate(stacked, axis=0), points)

    def pair(values, i):
        re = values[2 * i * BLOCKS : (2 * i + 1) * BLOCKS]
        im = values[(2 * i + 1) * BLOCKS : (2 * i + 2) * BLOCKS]
        return re[:, :HALF], re[:, HALF:], im[:, :HALF], im[:, HALF:]

    def spectrum(i):
        res, ims = [], []
        for part in (2 * i, 2 * i + 1):
            re_cos, re_sin, im_cos, im_sin = pair(spec, part)
            res.append(re_cos + im_sin)
            ims.append(im_cos - re_sin)
        return res, ims

    (p_re, p_im), (d_re, d_im), (h_re, h_im) = [spectrum(i) for i in range(3)]
    joined = []
    for e in range(2):
        joined += [h_re[e] * p_re[e] - h_im[e] * p_im[e], h_re[e] * p_im[e] + h_im[e] * p_re[e]]
    for e in range(2):
        joined += [d_re[e] * h_re[e] + d_im[e] * h_im[e], d_im[e] * h_re[e] - d_re[e] * h_im[e]]
    for e in range(2):
        joined += [d_re[e] * p_re[e] + d_im[e] * p_im[e], d_im[e] * p_re[e] - d_re[e] * p_im[e]]
    back = dot_right(jnp.concatenate(joined, axis=0), points)
    turned = []
    for i in range(3):
        re_cos, re_sin, im_cos, im_sin = pair(back, 2 * i)
        even_re, even_im = re_cos - im_sin, im_cos + re_sin
        re_cos, re_sin, im_cos, im_sin = pair(back, 2 * i + 1)
        re, im = re_cos - im_sin, im_cos + re_sin
        re, im = re * odd_cos - im * odd_sin, im * odd_cos + re * odd_sin
        b_re = jnp.concatenate([even_re + re, even_re - re], axis=1)
        b_im = jnp.concatenate([even_im + im, even_im - im], axis=1)
        turned.append(
            jnp.concatenate([b_re * cosine - b_im * sine, b_im * cosine + b_re * sine], axis=0)
        )
    result = dot_left(right, jnp.concatenate(turned, axis=1))
    conv_out = result[:, :SPAN] + direct * product
    dz = result[:, SPAN : 2 * SPAN] + direct * dw
    corr = result[:, 2 * SPAN :]

    grads = [grad * conv_out, dz * value, dz * key]
    odd = lax.rem(place // RUN, 2)

    def give(x, row):
        runs = [
            jnp.where(odd == 0, x[first : first + RUN], x[first + RUN : first + 2 * RUN])
            for first in range(0, BLOCKS, 2 * RUN)
        ]
        mine = jnp.concatenate(runs, axis=0)
        for side in range(2):
            out_ref[pl.ds(row + side, FILTERS, stride=ROWS), :] = mine[
                :, side * HALF : (side + 1) * HALF
            ]

    for b in range(3):
        g = grads[b]
        give(taps[b][0] * g + taps[b][1] * sooner(g, 1) + taps[b][2] * sooner(g, 2), 2 * b)
    give(corr, 6)
    sums = [whole_sum(grads[b] * moved[b][j]) for b in range(3) for j in range(TAPS)]
    sums.append(whole_sum(dw * product))
    lanes = lax.broadcasted_iota(jnp.int32, (1, HALF), 1)
    line = jnp.zeros((1, HALF), f32)
    for i, value in enumerate(sums):
        line = jnp.where(lanes == i, value, line)
    line = jnp.broadcast_to(line * TOTAL**-0.5, (FILTERS, HALF))
    out_ref[pl.ds(8, FILTERS, stride=ROWS), :] = line


def filter_kernel(data_ref, out_ref):
    for group in range(GROUPS):
        for side in range(2):
            first = ROWS * 4 * group + 6 + side
            out_ref[group, 4 * side : 4 * side + 4, :] = data_ref[pl.ds(first, 4, stride=ROWS), :]


def place_kernel(data_ref, partial_ref, grads_ref, skip_ref, short_ref, filter_ref):
    for b in range(3):
        for side in range(2):
            grads_ref[b, :, side * HALF : (side + 1) * HALF] = data_ref[
                pl.ds(2 * b + side, FILTERS, stride=ROWS), :
            ]
    sums = data_ref[pl.ds(8, FILTERS, stride=ROWS), :]
    padded = jnp.concatenate([sums, jnp.zeros((HALF - FILTERS, HALF), f32)], axis=0)
    flipped = padded.T[:, :FILTERS]
    for b in range(3):
        short_ref[b] = flipped[TAPS * b : TAPS * (b + 1), :]
    skip_ref[...] = flipped[9:10, :]
    total = partial_ref[0]
    for i in range(1, GROUPS):
        total = total + partial_ref[i]
    total = total * (TOTAL * GROUPS) ** -0.5
    for side in range(2):
        filter_ref[:, side * HALF : (side + 1) * HALF] = total[4 * side : 4 * side + 4, :]


vmem = pl.BlockSpec(memory_space=pltpu.VMEM)
hbm = pl.BlockSpec(memory_space=pltpu.HBM)
smem = pl.BlockSpec(memory_space=pltpu.SMEM)
params = pltpu.CompilerParams(vmem_limit_bytes=32 * 1024 * 1024)
pack_params = pltpu.CompilerParams(vmem_limit_bytes=56 * 1024 * 1024)


def like(shape, dtype=f32):
    return jax.ShapeDtypeStruct(shape, dtype)


def body(inputs, short_weights, filters, skip, grad_out):
    points, strip, turn = [jnp.asarray(values) for values in tables()]
    message = pl.pallas_call(
        pack_kernel,
        out_shape=like((BLOCKS, 4, 3 * HALF), bf16),
        in_specs=[hbm] * 3,
        out_specs=vmem,
        scratch_shapes=[
            pltpu.VMEM((3, FILTERS, SPAN), bf16),
            pltpu.VMEM((FILTERS, SPAN), bf16),
            pltpu.VMEM((FILTERS, SPAN), f32),
            pltpu.VMEM((BLOCKS, 4, 3 * HALF), f32),
            pltpu.SemaphoreType.DMA((3,)),
        ],
        compiler_params=pack_params,
    )(inputs, grad_out, filters)
    data = lax.all_to_all(message, "seq", split_axis=0, concat_axis=0, tiled=True)
    answer = pl.pallas_call(
        channel_kernel,
        out_shape=like((FILTERS * ROWS, HALF)),
        in_specs=[vmem, smem, smem] + [vmem] * 3,
        out_specs=vmem,
        scratch_shapes=[pltpu.VMEM((BLOCKS, 4, 3 * HALF), f32)],
        compiler_params=params,
    )(data, short_weights, skip, points, strip, turn)
    answer = lax.all_to_all(
        answer.reshape(FILTERS, 1, ROWS * HALF),
        "seq",
        split_axis=0,
        concat_axis=0,
        tiled=True,
        axis_index_groups=PARTNERS,
    ).reshape(FILTERS * ROWS, HALF)
    partial = pl.pallas_call(
        filter_kernel,
        out_shape=like((GROUPS, 8, HALF)),
        in_specs=[vmem],
        out_specs=vmem,
        compiler_params=params,
    )(answer)
    partial = lax.all_to_all(partial, "chan", split_axis=0, concat_axis=0, tiled=True)
    grads, skip_grad, short_grad, filter_grad = pl.pallas_call(
        place_kernel,
        out_shape=(
            like((3, FILTERS, SPAN)),
            like((1, FILTERS)),
            like((3, TAPS, FILTERS)),
            like((4, SPAN)),
        ),
        in_specs=[vmem] * 2,
        out_specs=(vmem,) * 4,
        compiler_params=params,
    )(answer, partial)
    return grads, filter_grad, skip_grad.reshape(FILTERS), short_grad


def solution(mesh):
    placed = (
        P(None, "chan", "seq"),
        P(None, None, "chan"),
        P(None, "seq"),
        P("chan"),
        P("chan", "seq"),
    )
    return jax.shard_map(
        body,
        mesh=mesh,
        in_specs=placed,
        out_specs=(P(None, "chan", "seq"), P("chan", "seq"), P("chan"), P(None, None, "chan")),
        check_vma=False,
    )
```

```python
import math

import jax
import jax.numpy as jnp
import numpy as np
from jax import lax
from jax.experimental import pallas as pl
from jax.experimental.pallas import tpu as pltpu
from jax.sharding import PartitionSpec as P

f32 = jnp.float32
bf16 = jnp.bfloat16
BLOCKS = 64
SPAN = 256
HALF = 128
FILTERS = 32
GROUPS = 8
TAPS = 3
ROWS = 9
RUN = 8
PARTNERS = [[16 * a + RUN * b + z for a in range(4) for z in range(RUN)] for b in range(2)]
TOTAL = BLOCKS * SPAN


def split_table(values):
    high = values.astype(jnp.bfloat16)
    low = (values - high.astype(np.float64)).astype(jnp.bfloat16)
    return high, low


def tables():
    rows = np.arange(BLOCKS)
    cols = np.arange(SPAN)
    odd = 4 * rows + 1
    outer = 2 * math.pi * (odd[:, None] * rows[None, :] % 256) / 256.0
    g = np.concatenate([np.cos(outer), -np.sin(outer)], axis=0)
    g_high, g_low = split_table(g)
    forward_rows = np.concatenate([g_high, g_high, g_low], axis=1)
    t = g.T / TOTAL
    t_high, t_low = split_table(t)
    inverse_rows = np.concatenate([t_high, t_low], axis=1)
    near = np.arange(HALF)
    inner = 2 * math.pi * (near[:, None] * near[None, :] % HALF) / HALF
    f = np.concatenate([np.cos(inner), np.sin(inner)], axis=1)
    f_high, f_low = split_table(f)
    points = np.concatenate([f_high, f_high, f_low], axis=0)
    strip = np.zeros((3 * BLOCKS, SPAN), dtype=jnp.bfloat16)
    strip[: 2 * BLOCKS, : 3 * BLOCKS] = forward_rows
    strip[2 * BLOCKS :] = inverse_rows
    eight = np.arange(8)
    coarse = 2 * math.pi * (32 * eight[:, None] * cols[None, :]) / (4.0 * TOTAL)
    fine = 2 * math.pi * ((4 * eight + 1)[:, None] * cols[None, :]) / (4.0 * TOTAL)
    step = 2 * math.pi * near / SPAN
    step = np.concatenate([np.cos(step), np.sin(step)])[None, :] * np.ones((8, 1))
    turn = np.concatenate([np.cos(coarse), np.sin(coarse), np.cos(fine), np.sin(fine), step])
    turn = turn.astype(np.float32)
    return points, strip, turn


def halves(x):
    high = x.astype(bf16)
    return high, (x - high.astype(f32)).astype(bf16)


def place_of(i):
    return i % 4, slice(i // 4 * HALF, (i // 4 + 1) * HALF)


def dot(a, b):
    return jnp.dot(a, b, preferred_element_type=f32)


def dot_left(table, x):
    high, low = halves(x)
    return dot(table, jnp.concatenate([high, low, high], axis=0))


def dot_right(x, table):
    high, low = halves(x)
    return dot(jnp.concatenate([high, low, high], axis=1), table)


def later(x, n):
    row = lax.broadcasted_iota(jnp.int32, x.shape, 0)
    col = lax.broadcasted_iota(jnp.int32, x.shape, 1)
    here = pltpu.roll(x, n, 1)
    above = jnp.where(row == 0, 0.0, pltpu.roll(here, 1, 0))
    return jnp.where(col < n, above, here)


def sooner(x, n):
    row = lax.broadcasted_iota(jnp.int32, x.shape, 0)
    col = lax.broadcasted_iota(jnp.int32, x.shape, 1)
    here = pltpu.roll(x, SPAN - n, 1)
    below = jnp.where(row == BLOCKS - 1, 0.0, pltpu.roll(here, BLOCKS - 1, 0))
    return jnp.where(col >= SPAN - n, below, here)


def pack_kernel(inputs_hbm, grad_hbm, filters_hbm, out_ref, inputs_ref, grad_ref, filters_ref, rows_ref, sems):
    copies = [
        pltpu.make_async_copy(source, target, sems.at[i])
        for i, (source, target) in enumerate(
            [(inputs_hbm, inputs_ref), (grad_hbm, grad_ref), (filters_hbm, filters_ref)]
        )
    ]
    for copy in copies:
        copy.start()
    for copy in copies:
        copy.wait()
    h = filters_ref[...]
    h_high = h.astype(bf16).astype(f32)
    parts = [inputs_ref[b].astype(f32) for b in range(3)]
    parts += [grad_ref[...].astype(f32), h_high, h - h_high]
    for i, part in enumerate(parts):
        for side in range(2):
            piece = part[:, side * HALF : (side + 1) * HALF]
            row, tile = place_of(2 * i + side)
            for first in range(0, BLOCKS, RUN):
                channel = first // (2 * RUN) * RUN
                rows_ref[first : first + RUN, row, tile] = piece[channel : channel + RUN]
    out_ref[...] = rows_ref[...].astype(bf16)


def whole_sum(x):
    return jnp.sum(jnp.sum(x, axis=0, keepdims=True), axis=1, keepdims=True)


def turns(turn_ref):
    cosines, sines = [], []
    fine_cos, fine_sin = turn_ref[16:24, :], turn_ref[24:32, :]
    for a in range(8):
        coarse_cos, coarse_sin = turn_ref[a : a + 1, :], turn_ref[8 + a : 9 + a, :]
        cosines.append(coarse_cos * fine_cos - coarse_sin * fine_sin)
        sines.append(coarse_sin * fine_cos + coarse_cos * fine_sin)
    return jnp.concatenate(cosines, axis=0), jnp.concatenate(sines, axis=0)


def channel_kernel(
    data_ref, taps_ref, skip_ref, points_ref, strip_ref, turn_ref, out_ref, rows_ref
):
    place = lax.axis_index("seq")
    channel = place // (2 * RUN) * RUN + lax.rem(place, RUN)
    rows_ref[...] = data_ref[...].astype(f32)

    def part(i):
        pieces = []
        for side in range(2):
            row, tile = place_of(2 * i + side)
            pieces.append(rows_ref[:, row, tile])
        return jnp.concatenate(pieces, axis=1)

    branch = [part(b) for b in range(3)]
    grad = part(3)
    h_high, h_low = part(4), part(5)
    taps = [[taps_ref[b, j, channel] for j in range(TAPS)] for b in range(3)]
    direct = skip_ref[channel]
    moved = [[branch[b]] + [later(branch[b], j) for j in range(1, TAPS)] for b in range(3)]
    query, key, value = [
        taps[b][0] * moved[b][0] + taps[b][1] * moved[b][1] + taps[b][2] * moved[b][2]
        for b in range(3)
    ]
    product = key * value
    dw = grad * query

    cosine, sine = turns(turn_ref)
    points = points_ref[...]
    odd_cos, odd_sin = turn_ref[32:33, :HALF], turn_ref[32:33, HALF:]
    left = strip_ref[: 2 * BLOCKS, : 3 * BLOCKS]
    right = strip_ref[2 * BLOCKS :, :]
    right = jnp.concatenate([right[:, :HALF], right], axis=1)
    start = dot_left(left, jnp.concatenate([product, dw, h_high + h_low], axis=1))
    stacked = []
    for i in range(3):
        re = start[:BLOCKS, i * SPAN : (i + 1) * SPAN]
        im = start[BLOCKS:, i * SPAN : (i + 1) * SPAN]
        re, im = re * cosine + im * sine, im * cosine - re * sine
        stacked += [re[:, :HALF] + re[:, HALF:], im[:, :HALF] + im[:, HALF:]]
        re, im = re[:, :HALF] - re[:, HALF:], im[:, :HALF] - im[:, HALF:]
        stacked += [re * odd_cos + im * odd_sin, im * odd_cos - re * odd_sin]
    spec = dot_right(jnp.concatenate(stacked, axis=0), points)

    def pair(values, i):
        re = values[2 * i * BLOCKS : (2 * i + 1) * BLOCKS]
        im = values[(2 * i + 1) * BLOCKS : (2 * i + 2) * BLOCKS]
        return re[:, :HALF], re[:, HALF:], im[:, :HALF], im[:, HALF:]

    def spectrum(i):
        res, ims = [], []
        for part in (2 * i, 2 * i + 1):
            re_cos, re_sin, im_cos, im_sin = pair(spec, part)
            res.append(re_cos + im_sin)
            ims.append(im_cos - re_sin)
        return res, ims

    (p_re, p_im), (d_re, d_im), (h_re, h_im) = [spectrum(i) for i in range(3)]
    joined = []
    for e in range(2):
        joined += [h_re[e] * p_re[e] - h_im[e] * p_im[e], h_re[e] * p_im[e] + h_im[e] * p_re[e]]
    for e in range(2):
        joined += [d_re[e] * h_re[e] + d_im[e] * h_im[e], d_im[e] * h_re[e] - d_re[e] * h_im[e]]
    for e in range(2):
        joined += [d_re[e] * p_re[e] + d_im[e] * p_im[e], d_im[e] * p_re[e] - d_re[e] * p_im[e]]
    back = dot_right(jnp.concatenate(joined, axis=0), points)
    turned = []
    for i in range(3):
        re_cos, re_sin, im_cos, im_sin = pair(back, 2 * i)
        even_re, even_im = re_cos - im_sin, im_cos + re_sin
        re_cos, re_sin, im_cos, im_sin = pair(back, 2 * i + 1)
        re, im = re_cos - im_sin, im_cos + re_sin
        re, im = re * odd_cos - im * odd_sin, im * odd_cos + re * odd_sin
        b_re = jnp.concatenate([even_re + re, even_re - re], axis=1)
        b_im = jnp.concatenate([even_im + im, even_im - im], axis=1)
        turned.append(
            jnp.concatenate([b_re * cosine - b_im * sine, b_im * cosine + b_re * sine], axis=0)
        )
    result = dot_left(right, jnp.concatenate(turned, axis=1))
    conv_out = result[:, :SPAN] + direct * product
    dz = result[:, SPAN : 2 * SPAN] + direct * dw
    corr = result[:, 2 * SPAN :]

    grads = [grad * conv_out, dz * value, dz * key]
    odd = lax.rem(place // RUN, 2)

    def give(x, row):
        runs = [
            jnp.where(odd == 0, x[first : first + RUN], x[first + RUN : first + 2 * RUN])
            for first in range(0, BLOCKS, 2 * RUN)
        ]
        mine = jnp.concatenate(runs, axis=0)
        for side in range(2):
            out_ref[pl.ds(row + side, FILTERS, stride=ROWS), :] = mine[
                :, side * HALF : (side + 1) * HALF
            ]

    for b in range(3):
        g = grads[b]
        give(taps[b][0] * g + taps[b][1] * sooner(g, 1) + taps[b][2] * sooner(g, 2), 2 * b)
    give(corr, 6)
    sums = [whole_sum(grads[b] * moved[b][j]) for b in range(3) for j in range(TAPS)]
    sums.append(whole_sum(dw * product))
    lanes = lax.broadcasted_iota(jnp.int32, (1, HALF), 1)
    line = jnp.zeros((1, HALF), f32)
    for i, value in enumerate(sums):
        line = jnp.where(lanes == i, value, line)
    line = jnp.broadcast_to(line * TOTAL**-0.5, (FILTERS, HALF))
    out_ref[pl.ds(8, FILTERS, stride=ROWS), :] = line


def filter_kernel(data_ref, out_ref):
    for group in range(GROUPS):
        for side in range(2):
            first = ROWS * 4 * group + 6 + side
            out_ref[group, 4 * side : 4 * side + 4, :] = data_ref[pl.ds(first, 4, stride=ROWS), :]


def place_kernel(data_ref, partial_ref, grads_ref, skip_ref, short_ref, filter_ref):
    for b in range(3):
        for side in range(2):
            grads_ref[b, :, side * HALF : (side + 1) * HALF] = data_ref[
                pl.ds(2 * b + side, FILTERS, stride=ROWS), :
            ]
    sums = data_ref[pl.ds(8, FILTERS, stride=ROWS), :]
    padded = jnp.concatenate([sums, jnp.zeros((HALF - FILTERS, HALF), f32)], axis=0)
    flipped = padded.T[:, :FILTERS]
    for b in range(3):
        short_ref[b] = flipped[TAPS * b : TAPS * (b + 1), :]
    skip_ref[...] = flipped[9:10, :]
    total = partial_ref[0]
    for i in range(1, GROUPS):
        total = total + partial_ref[i]
    total = total * (TOTAL * GROUPS) ** -0.5
    for side in range(2):
        filter_ref[:, side * HALF : (side + 1) * HALF] = total[4 * side : 4 * side + 4, :]


vmem = pl.BlockSpec(memory_space=pltpu.VMEM)
hbm = pl.BlockSpec(memory_space=pltpu.HBM)
smem = pl.BlockSpec(memory_space=pltpu.SMEM)
params = pltpu.CompilerParams(vmem_limit_bytes=32 * 1024 * 1024)


def like(shape, dtype=f32):
    return jax.ShapeDtypeStruct(shape, dtype)


def body(inputs, short_weights, filters, skip, grad_out):
    points, strip, turn = [jnp.asarray(values) for values in tables()]
    message = pl.pallas_call(
        pack_kernel,
        out_shape=like((BLOCKS, 4, 3 * HALF), bf16),
        in_specs=[hbm] * 3,
        out_specs=vmem,
        scratch_shapes=[
            pltpu.VMEM((3, FILTERS, SPAN), bf16),
            pltpu.VMEM((FILTERS, SPAN), bf16),
            pltpu.VMEM((FILTERS, SPAN), f32),
            pltpu.VMEM((BLOCKS, 4, 3 * HALF), f32),
            pltpu.SemaphoreType.DMA((3,)),
        ],
        compiler_params=params,
    )(*[pltpu.with_memory_space_constraint(x, pltpu.HBM) for x in (inputs, grad_out, filters)])
    data = lax.all_to_all(message, "seq", split_axis=0, concat_axis=0, tiled=True)
    answer = pl.pallas_call(
        channel_kernel,
        out_shape=like((FILTERS * ROWS, HALF)),
        in_specs=[vmem, smem, smem] + [vmem] * 3,
        out_specs=vmem,
        scratch_shapes=[pltpu.VMEM((BLOCKS, 4, 3 * HALF), f32)],
        compiler_params=params,
    )(data, short_weights, skip, points, strip, turn)
    answer = lax.all_to_all(
        answer.reshape(FILTERS, 1, ROWS * HALF),
        "seq",
        split_axis=0,
        concat_axis=0,
        tiled=True,
        axis_index_groups=PARTNERS,
    ).reshape(FILTERS * ROWS, HALF)
    partial = pl.pallas_call(
        filter_kernel,
        out_shape=like((GROUPS, 8, HALF)),
        in_specs=[vmem],
        out_specs=vmem,
        compiler_params=params,
    )(answer)
    partial = lax.all_to_all(partial, "chan", split_axis=0, concat_axis=0, tiled=True)
    grads, skip_grad, short_grad, filter_grad = pl.pallas_call(
        place_kernel,
        out_shape=(
            like((3, FILTERS, SPAN)),
            like((1, FILTERS)),
            like((3, TAPS, FILTERS)),
            like((4, SPAN)),
        ),
        in_specs=[vmem] * 2,
        out_specs=(vmem,) * 4,
        compiler_params=params,
    )(answer, partial)
    return grads, filter_grad, skip_grad.reshape(FILTERS), short_grad


def solution(mesh):
    placed = (
        P(None, "chan", "seq"),
        P(None, None, "chan"),
        P(None, "seq"),
        P("chan"),
        P("chan", "seq"),
    )
    return jax.shard_map(
        body,
        mesh=mesh,
        in_specs=placed,
        out_specs=(P(None, "chan", "seq"), P("chan", "seq"), P("chan"), P(None, None, "chan")),
        check_vma=False,
    )
```

```python
import math

import jax
import jax.numpy as jnp
import numpy as np
from jax import lax
from jax.experimental import pallas as pl
from jax.experimental.pallas import tpu as pltpu
from jax.sharding import PartitionSpec as P

f32 = jnp.float32
bf16 = jnp.bfloat16
BLOCKS = 64
SPAN = 256
HALF = 128
FILTERS = 32
GROUPS = 8
TAPS = 3
ROWS = 9
RUN = 8
PARTNERS = [[16 * x + RUN * b + z for x in range(4) for z in range(RUN)] for b in range(2)]


TOTAL = BLOCKS * SPAN


def is_far(g, owner):
    return abs(g // 2 - owner // 2) == 3


def owner_route():
    route = []
    for place in range(BLOCKS):
        for g in range(GROUPS):
            owner = place % RUN ^ g
            target = place ^ RUN if is_far(g, owner) else place
            route.append((place * GROUPS + g, target * GROUPS + owner))
    return route


def split_table(values):
    high = values.astype(jnp.bfloat16)
    low = (values - high.astype(np.float64)).astype(jnp.bfloat16)
    return high, low


def tables():
    rows = np.arange(BLOCKS)
    cols = np.arange(SPAN)
    odd = 4 * rows + 1
    outer = 2 * math.pi * (odd[:, None] * rows[None, :] % 256) / 256.0
    g = np.concatenate([np.cos(outer), -np.sin(outer)], axis=0)
    g_high, g_low = split_table(g)
    forward_rows = np.concatenate([g_high, g_high, g_low], axis=1)
    t = g.T / TOTAL
    t_high, t_low = split_table(t)
    inverse_rows = np.concatenate([t_high, t_low], axis=1)
    near = np.arange(HALF)
    inner = 2 * math.pi * (near[:, None] * near[None, :] % HALF) / HALF
    f = np.concatenate([np.cos(inner), np.sin(inner)], axis=1)
    f_high, f_low = split_table(f)
    points = np.concatenate([f_high, f_high, f_low], axis=0)
    strip = np.zeros((3 * BLOCKS, SPAN), dtype=jnp.bfloat16)
    strip[: 2 * BLOCKS, : 3 * BLOCKS] = forward_rows
    strip[2 * BLOCKS :] = inverse_rows
    eight = np.arange(8)
    coarse = 2 * math.pi * (32 * eight[:, None] * cols[None, :]) / (4.0 * TOTAL)
    fine = 2 * math.pi * ((4 * eight + 1)[:, None] * cols[None, :]) / (4.0 * TOTAL)
    step = 2 * math.pi * near / SPAN
    step = np.concatenate([np.cos(step), np.sin(step)])[None, :] * np.ones((8, 1))
    turn = np.concatenate([np.cos(coarse), np.sin(coarse), np.cos(fine), np.sin(fine), step])
    turn = turn.astype(np.float32)
    return points, strip, turn


def halves(x):
    high = x.astype(bf16)
    return high, (x - high.astype(f32)).astype(bf16)


def place_of(i):
    return i % 4, slice(i // 4 * HALF, (i // 4 + 1) * HALF)


def dot(a, b):
    return jnp.dot(a, b, preferred_element_type=f32)


def dot_left(table, x):
    high, low = halves(x)
    return dot(table, jnp.concatenate([high, low, high], axis=0))


def dot_right(x, table):
    high, low = halves(x)
    return dot(jnp.concatenate([high, low, high], axis=1), table)


def later(x, n):
    row = lax.broadcasted_iota(jnp.int32, x.shape, 0)
    col = lax.broadcasted_iota(jnp.int32, x.shape, 1)
    here = pltpu.roll(x, n, 1)
    above = jnp.where(row == 0, 0.0, pltpu.roll(here, 1, 0))
    return jnp.where(col < n, above, here)


def sooner(x, n):
    row = lax.broadcasted_iota(jnp.int32, x.shape, 0)
    col = lax.broadcasted_iota(jnp.int32, x.shape, 1)
    here = pltpu.roll(x, SPAN - n, 1)
    below = jnp.where(row == BLOCKS - 1, 0.0, pltpu.roll(here, BLOCKS - 1, 0))
    return jnp.where(col >= SPAN - n, below, here)


def pack_kernel(inputs_hbm, grad_hbm, filters_hbm, out_ref, inputs_ref, grad_ref, filters_ref, rows_ref, short_ref, sems):
    copies = [
        pltpu.make_async_copy(source, target, sems.at[i])
        for i, (source, target) in enumerate(
            [(inputs_hbm, inputs_ref), (grad_hbm, grad_ref), (filters_hbm, filters_ref)]
        )
    ]
    for copy in copies:
        copy.start()
    for copy in copies:
        copy.wait()
    h = filters_ref[...]
    h_high = h.astype(bf16).astype(f32)
    parts = [inputs_ref[b].astype(f32) for b in range(3)]
    parts += [grad_ref[...].astype(f32), h_high, h - h_high]
    for i, part in enumerate(parts):
        for side in range(2):
            row, tile = place_of(2 * i + side)
            rows_ref[:, row, tile] = part[:, side * HALF : (side + 1) * HALF]
    short_ref[...] = rows_ref[...].astype(bf16)
    g = lax.axis_index("chan")
    for place in range(BLOCKS):
        out_ref[place] = short_ref[4 * jnp.bitwise_xor(g, place % RUN) + place // (2 * RUN)]


def whole_sum(x):
    return jnp.sum(jnp.sum(x, axis=0, keepdims=True), axis=1, keepdims=True)


def turns(turn_ref):
    cosines, sines = [], []
    fine_cos, fine_sin = turn_ref[16:24, :], turn_ref[24:32, :]
    for a in range(8):
        coarse_cos, coarse_sin = turn_ref[a : a + 1, :], turn_ref[8 + a : 9 + a, :]
        cosines.append(coarse_cos * fine_cos - coarse_sin * fine_sin)
        sines.append(coarse_sin * fine_cos + coarse_cos * fine_sin)
    return jnp.concatenate(cosines, axis=0), jnp.concatenate(sines, axis=0)


def seat():
    place, g = lax.axis_index("seq"), lax.axis_index("chan")
    owner = jnp.bitwise_xor(lax.rem(place, RUN), g)
    return g, owner, 4 * owner + place // (2 * RUN), lax.rem(place // RUN, 2)


def unpack(data_ref, rows_ref):
    rows_ref[...] = data_ref[...].astype(f32)
    parts = []
    for i in range(6):
        pieces = []
        for side in range(2):
            row, tile = place_of(2 * i + side)
            pieces.append(rows_ref[:, row, tile])
        parts.append(jnp.concatenate(pieces, axis=1))
    return parts


def mix(branch, taps):
    moved = [[x] + [later(x, j) for j in range(1, TAPS)] for x in branch]
    mixed = [
        taps[b][0] * moved[b][0] + taps[b][1] * moved[b][1] + taps[b][2] * moved[b][2]
        for b in range(3)
    ]
    return moved, mixed


def constants(strip_ref, turn_ref):
    left = strip_ref[: 2 * BLOCKS, : 3 * BLOCKS]
    right = strip_ref[2 * BLOCKS :, :]
    right = jnp.concatenate([right[:, :HALF], right], axis=1)
    odd = turn_ref[32:33, :HALF], turn_ref[32:33, HALF:]
    return left, right, turns(turn_ref), odd


def pair(values, i):
    re = values[2 * i * BLOCKS : (2 * i + 1) * BLOCKS]
    im = values[(2 * i + 1) * BLOCKS : (2 * i + 2) * BLOCKS]
    return re[:, :HALF], re[:, HALF:], im[:, :HALF], im[:, HALF:]


def spectra(signals, points, left, turn, odd):
    cosine, sine = turn
    odd_cos, odd_sin = odd
    start = dot_left(left, jnp.concatenate(signals, axis=1))
    stacked = []
    for i in range(len(signals)):
        re = start[:BLOCKS, i * SPAN : (i + 1) * SPAN]
        im = start[BLOCKS:, i * SPAN : (i + 1) * SPAN]
        re, im = re * cosine + im * sine, im * cosine - re * sine
        stacked += [re[:, :HALF] + re[:, HALF:], im[:, :HALF] + im[:, HALF:]]
        re, im = re[:, :HALF] - re[:, HALF:], im[:, :HALF] - im[:, HALF:]
        stacked += [re * odd_cos + im * odd_sin, im * odd_cos - re * odd_sin]
    values = dot_right(jnp.concatenate(stacked, axis=0), points)
    results = []
    for i in range(2 * len(signals)):
        re_cos, re_sin, im_cos, im_sin = pair(values, i)
        results.append((re_cos + im_sin, im_cos - re_sin))
    return [results[2 * i : 2 * i + 2] for i in range(len(signals))]


def times(a, b):
    return a[0] * b[0] - a[1] * b[1], a[0] * b[1] + a[1] * b[0]


def times_conj(a, b):
    return a[0] * b[0] + a[1] * b[1], a[1] * b[0] - a[0] * b[1]


def inverse(spectrums, points, right, turn, odd):
    cosine, sine = turn
    odd_cos, odd_sin = odd
    joined = [x for spectrum in spectrums for part in spectrum for x in part]
    back = dot_right(jnp.concatenate(joined, axis=0), points)
    turned = []
    for i in range(len(spectrums)):
        re_cos, re_sin, im_cos, im_sin = pair(back, 2 * i)
        even_re, even_im = re_cos - im_sin, im_cos + re_sin
        re_cos, re_sin, im_cos, im_sin = pair(back, 2 * i + 1)
        re, im = re_cos - im_sin, im_cos + re_sin
        re, im = re * odd_cos - im * odd_sin, im * odd_cos + re * odd_sin
        b_re = jnp.concatenate([even_re + re, even_re - re], axis=1)
        b_im = jnp.concatenate([even_im + im, even_im - im], axis=1)
        turned.append(
            jnp.concatenate([b_re * cosine - b_im * sine, b_im * cosine + b_re * sine], axis=0)
        )
    return dot_left(right, jnp.concatenate(turned, axis=1))


def every_second_run(x, b):
    runs = [
        jnp.where(b == 0, x[first : first + RUN], x[first + RUN : first + 2 * RUN])
        for first in range(0, BLOCKS, 2 * RUN)
    ]
    return jnp.concatenate(runs, axis=0)


def corr_kernel(
    data_ref, taps_ref, skip_ref, points_ref, strip_ref, turn_ref, corr_ref, spec_ref, rows_ref
):
    g, owner, channel, b_own = seat()
    parts = unpack(data_ref, rows_ref)
    taps = [[taps_ref[b, j, channel] for j in range(TAPS)] for b in range(3)]
    _, (query, key, value) = mix(parts[:3], taps)
    product, dw = key * value, parts[3] * query
    left, right, turn, odd = constants(strip_ref, turn_ref)
    points = points_ref[...]
    p, d = spectra([product, dw], points, left, turn, odd)
    for i, x in enumerate([x for spectrum in (p, d) for part in spectrum for x in part]):
        spec_ref[i * BLOCKS : (i + 1) * BLOCKS, :] = x
    corr = inverse([[times_conj(d[e], p[e]) for e in range(2)]], points, right, turn, odd)
    b_there = jnp.where(is_far(g, owner), 1 - b_own, b_own)
    corr = every_second_run(corr, b_there)
    for side in range(2):
        corr_ref[side * FILTERS : (side + 1) * FILTERS, :] = corr[:, side * HALF : (side + 1) * HALF]


def channel_kernel(
    data_ref, taps_ref, skip_ref, points_ref, strip_ref, turn_ref, spec_ref, out_ref, rows_ref
):
    _, _, channel, b_own = seat()
    parts = unpack(data_ref, rows_ref)
    grad, h = parts[3], parts[4] + parts[5]
    taps = [[taps_ref[b, j, channel] for j in range(TAPS)] for b in range(3)]
    direct = skip_ref[channel]
    moved, (query, key, value) = mix(parts[:3], taps)
    product, dw = key * value, grad * query
    left, right, turn, odd = constants(strip_ref, turn_ref)
    points = points_ref[...]
    (h_spec,) = spectra([h], points, left, turn, odd)
    held = [spec_ref[i * BLOCKS : (i + 1) * BLOCKS, :] for i in range(8)]
    p = [(held[0], held[1]), (held[2], held[3])]
    d = [(held[4], held[5]), (held[6], held[7])]
    result = inverse(
        [
            [times(h_spec[e], p[e]) for e in range(2)],
            [times_conj(d[e], h_spec[e]) for e in range(2)],
        ],
        points,
        right,
        turn,
        odd,
    )
    conv_out = result[:, :SPAN] + direct * product
    dz = result[:, SPAN:] + direct * dw

    grads = [grad * conv_out, dz * value, dz * key]
    for b in range(3):
        g = grads[b]
        total = taps[b][0] * g + taps[b][1] * sooner(g, 1) + taps[b][2] * sooner(g, 2)
        mine = every_second_run(total, b_own)
        for side in range(2):
            out_ref[pl.ds(2 * b + side, FILTERS, stride=ROWS), :] = mine[
                :, side * HALF : (side + 1) * HALF
            ]
    for row in (6, 7):
        out_ref[pl.ds(row, FILTERS, stride=ROWS), :] = jnp.zeros((FILTERS, HALF), f32)
    sums = [whole_sum(grads[b] * moved[b][j]) for b in range(3) for j in range(TAPS)]
    sums.append(whole_sum(dw * product))
    lanes = lax.broadcasted_iota(jnp.int32, (1, HALF), 1)
    line = jnp.zeros((1, HALF), f32)
    for i, value in enumerate(sums):
        line = jnp.where(lanes == i, value, line)
    line = jnp.broadcast_to(line * TOTAL**-0.5, (FILTERS, HALF))
    out_ref[pl.ds(8, FILTERS, stride=ROWS), :] = line


def merge_kernel(answer_ref, corr_ref, out_ref):
    out_ref[...] = answer_ref[...]
    for side in range(2):
        out_ref[pl.ds(6 + side, FILTERS, stride=ROWS), :] = corr_ref[
            side * FILTERS : (side + 1) * FILTERS, :
        ]


def place_kernel(data_ref, grads_ref, skip_ref, short_ref, filter_ref, sums_ref):
    g = lax.axis_index("chan")
    for owner in range(GROUPS):
        first = ROWS * jnp.bitwise_xor(g, owner)
        rows = slice(4 * owner, 4 * owner + 4)
        for b in range(3):
            for side in range(2):
                grads_ref[b, rows, side * HALF : (side + 1) * HALF] = data_ref[
                    pl.ds(first + (2 * b + side), 4, stride=RUN * ROWS), :
                ]
        sums_ref[rows, :] = data_ref[pl.ds(first + 8, 4, stride=RUN * ROWS), :]
    padded = jnp.concatenate([sums_ref[...], jnp.zeros((HALF - FILTERS, HALF), f32)], axis=0)
    flipped = padded.T[:, :FILTERS]
    for b in range(3):
        short_ref[b] = flipped[TAPS * b : TAPS * (b + 1), :]
    skip_ref[...] = flipped[9:10, :]
    for x in range(4):
        for side in range(2):
            terms = data_ref[pl.ds(x * RUN * ROWS + 6 + side, RUN, stride=ROWS), :]
            total = jnp.sum(terms, axis=0, keepdims=True) * (TOTAL * GROUPS) ** -0.5
            filter_ref[x : x + 1, side * HALF : (side + 1) * HALF] = total


vmem = pl.BlockSpec(memory_space=pltpu.VMEM)
hbm = pl.BlockSpec(memory_space=pltpu.HBM)
smem = pl.BlockSpec(memory_space=pltpu.SMEM)
params = pltpu.CompilerParams(vmem_limit_bytes=32 * 1024 * 1024)


def like(shape, dtype=f32):
    return jax.ShapeDtypeStruct(shape, dtype)


def body(inputs, short_weights, filters, skip, grad_out):
    points, strip, turn = [jnp.asarray(values) for values in tables()]
    message = pl.pallas_call(
        pack_kernel,
        out_shape=like((BLOCKS, 4, 3 * HALF), bf16),
        in_specs=[hbm] * 3,
        out_specs=vmem,
        scratch_shapes=[
            pltpu.VMEM((3, FILTERS, SPAN), bf16),
            pltpu.VMEM((FILTERS, SPAN), bf16),
            pltpu.VMEM((FILTERS, SPAN), f32),
            pltpu.VMEM((FILTERS, 4, 3 * HALF), f32),
            pltpu.VMEM((FILTERS, 4, 3 * HALF), bf16),
            pltpu.SemaphoreType.DMA((3,)),
        ],
        compiler_params=params,
    )(*[pltpu.with_memory_space_constraint(x, pltpu.HBM) for x in (inputs, grad_out, filters)])
    data = lax.all_to_all(message, "seq", split_axis=0, concat_axis=0, tiled=True)
    corr, spec = pl.pallas_call(
        corr_kernel,
        out_shape=(like((BLOCKS, HALF)), like((8 * BLOCKS, HALF))),
        in_specs=[vmem, smem, smem] + [vmem] * 3,
        out_specs=(vmem,) * 2,
        scratch_shapes=[pltpu.VMEM((BLOCKS, 4, 3 * HALF), f32)],
        compiler_params=params,
    )(data, short_weights, skip, points, strip, turn)
    corr = lax.ppermute(corr, ("seq", "chan"), owner_route())
    answer = pl.pallas_call(
        channel_kernel,
        out_shape=like((FILTERS * ROWS, HALF)),
        in_specs=[vmem, smem, smem] + [vmem] * 4,
        out_specs=vmem,
        scratch_shapes=[pltpu.VMEM((BLOCKS, 4, 3 * HALF), f32)],
        compiler_params=params,
        cost_estimate=pl.CostEstimate(flops=10**9, bytes_accessed=4 * 10**6, transcendentals=0),
    )(data, short_weights, skip, points, strip, turn, spec)
    answer = pl.pallas_call(
        merge_kernel,
        out_shape=like((FILTERS * ROWS, HALF)),
        in_specs=[vmem] * 2,
        out_specs=vmem,
        compiler_params=params,
    )(answer, corr)
    answer = lax.all_to_all(
        answer.reshape(FILTERS, 1, ROWS * HALF),
        "seq",
        split_axis=0,
        concat_axis=0,
        tiled=True,
        axis_index_groups=PARTNERS,
    ).reshape(FILTERS * ROWS, HALF)
    grads, skip_grad, short_grad, filter_grad = pl.pallas_call(
        place_kernel,
        out_shape=(
            like((3, FILTERS, SPAN)),
            like((1, FILTERS)),
            like((3, TAPS, FILTERS)),
            like((4, SPAN)),
        ),
        in_specs=[vmem],
        out_specs=(vmem,) * 4,
        scratch_shapes=[pltpu.VMEM((FILTERS, HALF), f32)],
        compiler_params=params,
    )(answer)
    return grads, filter_grad, skip_grad.reshape(FILTERS), short_grad


def solution(mesh):
    placed = (
        P(None, "chan", "seq"),
        P(None, None, "chan"),
        P(None, "seq"),
        P("chan"),
        P("chan", "seq"),
    )
    return jax.shard_map(
        body,
        mesh=mesh,
        in_specs=placed,
        out_specs=(P(None, "chan", "seq"), P("chan", "seq"), P("chan"), P(None, None, "chan")),
        check_vma=False,
    )
```

```python
import math

import jax
import jax.numpy as jnp
import numpy as np
from jax import lax
from jax.experimental import pallas as pl
from jax.experimental.pallas import tpu as pltpu
from jax.sharding import PartitionSpec as P

f32 = jnp.float32
bf16 = jnp.bfloat16
BLOCKS = 64
SPAN = 256
HALF = 128
FILTERS = 32
GROUPS = 8
TAPS = 3
ROWS = 9
RUN = 8
PARTNERS = [[16 * x + RUN * b + z for x in range(4) for z in range(RUN)] for b in range(2)]


TOTAL = BLOCKS * SPAN


def is_far(g, owner):
    return abs(g // 2 - owner // 2) == 3


def owner_route():
    route = []
    for place in range(BLOCKS):
        for g in range(GROUPS):
            owner = place % RUN ^ g
            target = place ^ RUN if is_far(g, owner) else place
            route.append((place * GROUPS + g, target * GROUPS + owner))
    return route


def split_table(values):
    high = values.astype(jnp.bfloat16)
    low = (values - high.astype(np.float64)).astype(jnp.bfloat16)
    return high, low


def tables():
    rows = np.arange(BLOCKS)
    cols = np.arange(SPAN)
    odd = 4 * rows + 1
    outer = 2 * math.pi * (odd[:, None] * rows[None, :] % 256) / 256.0
    g = np.concatenate([np.cos(outer), -np.sin(outer)], axis=0)
    g_high, g_low = split_table(g)
    forward_rows = np.concatenate([g_high, g_high, g_low], axis=1)
    t = g.T / TOTAL
    t_high, t_low = split_table(t)
    inverse_rows = np.concatenate([t_high, t_low], axis=1)
    near = np.arange(HALF)
    inner = 2 * math.pi * (near[:, None] * near[None, :] % HALF) / HALF
    f = np.concatenate([np.cos(inner), np.sin(inner)], axis=1)
    f_high, f_low = split_table(f)
    points = np.concatenate([f_high, f_high, f_low], axis=0)
    strip = np.zeros((3 * BLOCKS, SPAN), dtype=jnp.bfloat16)
    strip[: 2 * BLOCKS, : 3 * BLOCKS] = forward_rows
    strip[2 * BLOCKS :] = inverse_rows
    full = 2 * math.pi * (odd[:, None] * cols[None, :]) / (4.0 * TOTAL)
    step = 2 * math.pi * near / SPAN
    step = np.concatenate([np.cos(step), np.sin(step)])[None, :] * np.ones((8, 1))
    turn = np.concatenate([np.cos(full), np.sin(full), step]).astype(np.float32)
    return points, strip, turn


def halves(x):
    high = x.astype(bf16)
    return high, (x - high.astype(f32)).astype(bf16)


def place_of(i):
    return i % 4, slice(i // 4 * HALF, (i // 4 + 1) * HALF)


def dot(a, b):
    return jnp.dot(a, b, preferred_element_type=f32)


def dot_left(table, x):
    high, low = halves(x)
    return dot(table, jnp.concatenate([high, low, high], axis=0))


def dot_right(x, table):
    high, low = halves(x)
    return dot(jnp.concatenate([high, low, high], axis=1), table)


def later(x, n):
    row = lax.broadcasted_iota(jnp.int32, x.shape, 0)
    col = lax.broadcasted_iota(jnp.int32, x.shape, 1)
    here = pltpu.roll(x, n, 1)
    above = jnp.where(row == 0, 0.0, pltpu.roll(here, 1, 0))
    return jnp.where(col < n, above, here)


def sooner(x, n):
    row = lax.broadcasted_iota(jnp.int32, x.shape, 0)
    col = lax.broadcasted_iota(jnp.int32, x.shape, 1)
    here = pltpu.roll(x, SPAN - n, 1)
    below = jnp.where(row == BLOCKS - 1, 0.0, pltpu.roll(here, BLOCKS - 1, 0))
    return jnp.where(col >= SPAN - n, below, here)


def pack_kernel(inputs_hbm, grad_hbm, filters_hbm, out_ref, inputs_ref, grad_ref, filters_ref, rows_ref, short_ref, sems):
    copies = [
        pltpu.make_async_copy(source, target, sems.at[i])
        for i, (source, target) in enumerate(
            [(inputs_hbm, inputs_ref), (grad_hbm, grad_ref), (filters_hbm, filters_ref)]
        )
    ]
    for copy in copies:
        copy.start()
    for copy in copies:
        copy.wait()
    h = filters_ref[...]
    h_high = h.astype(bf16).astype(f32)
    parts = [inputs_ref[b].astype(f32) for b in range(3)]
    parts += [grad_ref[...].astype(f32), h_high, h - h_high]
    for i, part in enumerate(parts):
        for side in range(2):
            row, tile = place_of(2 * i + side)
            rows_ref[:, row, tile] = part[:, side * HALF : (side + 1) * HALF]
    short_ref[...] = rows_ref[...].astype(bf16)
    g = lax.axis_index("chan")
    for place in range(BLOCKS):
        out_ref[place] = short_ref[4 * jnp.bitwise_xor(g, place % RUN) + place // (2 * RUN)]


def whole_sum(x):
    return jnp.sum(jnp.sum(x, axis=0, keepdims=True), axis=1, keepdims=True)


def seat():
    place, g = lax.axis_index("seq"), lax.axis_index("chan")
    owner = jnp.bitwise_xor(lax.rem(place, RUN), g)
    return g, owner, 4 * owner + place // (2 * RUN), lax.rem(place // RUN, 2)


def own_taps(taps_ref, channel):
    lane = lax.broadcasted_iota(jnp.int32, taps_ref.shape, 2)
    own = jnp.sum(jnp.where(lane == channel, taps_ref[...], 0.0), axis=2, keepdims=True)
    return [[own[b, j : j + 1, :] for j in range(TAPS)] for b in range(3)]


def unpack(data_ref, rows_ref, count):
    width = count // 2 * HALF
    rows_ref[:, :, :width] = data_ref[:, :, :width].astype(f32)
    parts = []
    for i in range(count):
        pieces = []
        for side in range(2):
            row, tile = place_of(2 * i + side)
            pieces.append(rows_ref[:, row, tile])
        parts.append(jnp.concatenate(pieces, axis=1))
    return parts


def mix(branch, taps):
    moved = [[x] + [later(x, j) for j in range(1, TAPS)] for x in branch]
    mixed = [
        taps[b][0] * moved[b][0] + taps[b][1] * moved[b][1] + taps[b][2] * moved[b][2]
        for b in range(3)
    ]
    return moved, mixed


def constants(strip_ref, turn_ref):
    left = strip_ref[: 2 * BLOCKS, : 3 * BLOCKS]
    right = strip_ref[2 * BLOCKS :, :]
    right = jnp.concatenate([right[:, :HALF], right], axis=1)
    last = 2 * BLOCKS
    odd = turn_ref[last : last + 1, :HALF], turn_ref[last : last + 1, HALF:]
    return left, right, (turn_ref[:BLOCKS, :], turn_ref[BLOCKS:last, :]), odd


def pair(values, i):
    re = values[2 * i * BLOCKS : (2 * i + 1) * BLOCKS]
    im = values[(2 * i + 1) * BLOCKS : (2 * i + 2) * BLOCKS]
    return re[:, :HALF], re[:, HALF:], im[:, :HALF], im[:, HALF:]


def spectra(signals, points, left, turn, odd):
    cosine, sine = turn
    odd_cos, odd_sin = odd
    start = dot_left(left, jnp.concatenate(signals, axis=1))
    stacked = []
    for i in range(len(signals)):
        re = start[:BLOCKS, i * SPAN : (i + 1) * SPAN]
        im = start[BLOCKS:, i * SPAN : (i + 1) * SPAN]
        re, im = re * cosine + im * sine, im * cosine - re * sine
        stacked += [re[:, :HALF] + re[:, HALF:], im[:, :HALF] + im[:, HALF:]]
        re, im = re[:, :HALF] - re[:, HALF:], im[:, :HALF] - im[:, HALF:]
        stacked += [re * odd_cos + im * odd_sin, im * odd_cos - re * odd_sin]
    values = dot_right(jnp.concatenate(stacked, axis=0), points)
    results = []
    for i in range(2 * len(signals)):
        re_cos, re_sin, im_cos, im_sin = pair(values, i)
        results.append((re_cos + im_sin, im_cos - re_sin))
    return [results[2 * i : 2 * i + 2] for i in range(len(signals))]


def times(a, b):
    return a[0] * b[0] - a[1] * b[1], a[0] * b[1] + a[1] * b[0]


def times_conj(a, b):
    return a[0] * b[0] + a[1] * b[1], a[1] * b[0] - a[0] * b[1]


def inverse(spectrums, points, right, turn, odd):
    cosine, sine = turn
    odd_cos, odd_sin = odd
    joined = [x for spectrum in spectrums for part in spectrum for x in part]
    back = dot_right(jnp.concatenate(joined, axis=0), points)
    turned = []
    for i in range(len(spectrums)):
        re_cos, re_sin, im_cos, im_sin = pair(back, 2 * i)
        even_re, even_im = re_cos - im_sin, im_cos + re_sin
        re_cos, re_sin, im_cos, im_sin = pair(back, 2 * i + 1)
        re, im = re_cos - im_sin, im_cos + re_sin
        re, im = re * odd_cos - im * odd_sin, im * odd_cos + re * odd_sin
        b_re = jnp.concatenate([even_re + re, even_re - re], axis=1)
        b_im = jnp.concatenate([even_im + im, even_im - im], axis=1)
        turned.append(
            jnp.concatenate([b_re * cosine - b_im * sine, b_im * cosine + b_re * sine], axis=0)
        )
    return dot_left(right, jnp.concatenate(turned, axis=1))


def every_second_run(x, b):
    runs = [
        jnp.where(b == 0, x[first : first + RUN], x[first + RUN : first + 2 * RUN])
        for first in range(0, BLOCKS, 2 * RUN)
    ]
    return jnp.concatenate(runs, axis=0)


def corr_kernel(
    data_ref, taps_ref, skip_ref, points_ref, strip_ref, turn_ref, corr_ref, spec_ref, rows_ref
):
    g, owner, channel, b_own = seat()
    parts = unpack(data_ref, rows_ref, 4)
    taps = own_taps(taps_ref, channel)
    _, (query, key, value) = mix(parts[:3], taps)
    product, dw = key * value, parts[3] * query
    left, right, turn, odd = constants(strip_ref, turn_ref)
    points = points_ref[...]
    p, d = spectra([product, dw], points, left, turn, odd)
    for i, x in enumerate([x for spectrum in (p, d) for part in spectrum for x in part]):
        spec_ref[i * BLOCKS : (i + 1) * BLOCKS, :] = x
    corr = inverse([[times_conj(d[e], p[e]) for e in range(2)]], points, right, turn, odd)
    b_there = jnp.where(is_far(g, owner), 1 - b_own, b_own)
    corr = every_second_run(corr, b_there)
    for side in range(2):
        corr_ref[side * FILTERS : (side + 1) * FILTERS, :] = corr[:, side * HALF : (side + 1) * HALF]


def channel_kernel(
    data_ref, taps_ref, skip_ref, points_ref, strip_ref, turn_ref, spec_ref, out_ref, rows_ref
):
    _, _, channel, b_own = seat()
    parts = unpack(data_ref, rows_ref, 6)
    grad, h = parts[3], parts[4] + parts[5]
    taps = own_taps(taps_ref, channel)
    lane = lax.broadcasted_iota(jnp.int32, (1, FILTERS), 1)
    line = skip_ref[...].reshape(1, FILTERS)
    direct = jnp.sum(jnp.where(lane == channel, line, 0.0), axis=1, keepdims=True)
    moved, (query, key, value) = mix(parts[:3], taps)
    product, dw = key * value, grad * query
    left, right, turn, odd = constants(strip_ref, turn_ref)
    points = points_ref[...]
    (h_spec,) = spectra([h], points, left, turn, odd)
    held = [spec_ref[i * BLOCKS : (i + 1) * BLOCKS, :] for i in range(8)]
    p = [(held[0], held[1]), (held[2], held[3])]
    d = [(held[4], held[5]), (held[6], held[7])]
    result = inverse(
        [
            [times(h_spec[e], p[e]) for e in range(2)],
            [times_conj(d[e], h_spec[e]) for e in range(2)],
        ],
        points,
        right,
        turn,
        odd,
    )
    conv_out = result[:, :SPAN] + direct * product
    dz = result[:, SPAN:] + direct * dw

    grads = [grad * conv_out, dz * value, dz * key]
    for b in range(3):
        g = grads[b]
        total = taps[b][0] * g + taps[b][1] * sooner(g, 1) + taps[b][2] * sooner(g, 2)
        mine = every_second_run(total, b_own)
        for side in range(2):
            out_ref[pl.ds(2 * b + side, FILTERS, stride=ROWS), :] = mine[
                :, side * HALF : (side + 1) * HALF
            ]
    for row in (6, 7):
        out_ref[pl.ds(row, FILTERS, stride=ROWS), :] = jnp.zeros((FILTERS, HALF), f32)
    sums = [whole_sum(grads[b] * moved[b][j]) for b in range(3) for j in range(TAPS)]
    sums.append(whole_sum(dw * product))
    lanes = lax.broadcasted_iota(jnp.int32, (1, HALF), 1)
    line = jnp.zeros((1, HALF), f32)
    for i, value in enumerate(sums):
        line = jnp.where(lanes == i, value, line)
    line = jnp.broadcast_to(line * TOTAL**-0.5, (FILTERS, HALF))
    out_ref[pl.ds(8, FILTERS, stride=ROWS), :] = line


def merge_kernel(answer_ref, corr_ref, out_ref):
    out_ref[...] = answer_ref[...]
    for side in range(2):
        out_ref[pl.ds(6 + side, FILTERS, stride=ROWS), :] = corr_ref[
            side * FILTERS : (side + 1) * FILTERS, :
        ]


def place_kernel(data_ref, grads_ref, skip_ref, short_ref, filter_ref, sums_ref):
    g = lax.axis_index("chan")
    for owner in range(GROUPS):
        first = ROWS * jnp.bitwise_xor(g, owner)
        rows = slice(4 * owner, 4 * owner + 4)
        for b in range(3):
            for side in range(2):
                grads_ref[b, rows, side * HALF : (side + 1) * HALF] = data_ref[
                    pl.ds(first + (2 * b + side), 4, stride=RUN * ROWS), :
                ]
        sums_ref[rows, :] = data_ref[pl.ds(first + 8, 4, stride=RUN * ROWS), :]
    padded = jnp.concatenate([sums_ref[...], jnp.zeros((HALF - FILTERS, HALF), f32)], axis=0)
    flipped = padded.T[:, :FILTERS]
    for b in range(3):
        short_ref[b] = flipped[TAPS * b : TAPS * (b + 1), :]
    skip_ref[...] = flipped[9:10, :]
    for x in range(4):
        for side in range(2):
            terms = data_ref[pl.ds(x * RUN * ROWS + 6 + side, RUN, stride=ROWS), :]
            total = jnp.sum(terms, axis=0, keepdims=True) * (TOTAL * GROUPS) ** -0.5
            filter_ref[x : x + 1, side * HALF : (side + 1) * HALF] = total


vmem = pl.BlockSpec(memory_space=pltpu.VMEM)
hbm = pl.BlockSpec(memory_space=pltpu.HBM)
params = pltpu.CompilerParams(vmem_limit_bytes=32 * 1024 * 1024)


def like(shape, dtype=f32):
    return jax.ShapeDtypeStruct(shape, dtype)


def body(inputs, short_weights, filters, skip, grad_out):
    points, strip, turn = [jnp.asarray(values) for values in tables()]
    message = pl.pallas_call(
        pack_kernel,
        out_shape=like((BLOCKS, 4, 3 * HALF), bf16),
        in_specs=[hbm] * 3,
        out_specs=vmem,
        scratch_shapes=[
            pltpu.VMEM((3, FILTERS, SPAN), bf16),
            pltpu.VMEM((FILTERS, SPAN), bf16),
            pltpu.VMEM((FILTERS, SPAN), f32),
            pltpu.VMEM((FILTERS, 4, 3 * HALF), f32),
            pltpu.VMEM((FILTERS, 4, 3 * HALF), bf16),
            pltpu.SemaphoreType.DMA((3,)),
        ],
        compiler_params=params,
    )(*[pltpu.with_memory_space_constraint(x, pltpu.HBM) for x in (inputs, grad_out, filters)])
    data = lax.all_to_all(message, "seq", split_axis=0, concat_axis=0, tiled=True)
    corr, spec = pl.pallas_call(
        corr_kernel,
        out_shape=(like((BLOCKS, HALF)), like((8 * BLOCKS, HALF))),
        in_specs=[vmem] * 6,
        out_specs=(vmem,) * 2,
        scratch_shapes=[pltpu.VMEM((BLOCKS, 4, 3 * HALF), f32)],
        compiler_params=params,
    )(data, short_weights, skip, points, strip, turn)
    corr = lax.ppermute(corr, ("seq", "chan"), owner_route())
    answer = pl.pallas_call(
        channel_kernel,
        out_shape=like((FILTERS * ROWS, HALF)),
        in_specs=[vmem] * 7,
        out_specs=vmem,
        scratch_shapes=[pltpu.VMEM((BLOCKS, 4, 3 * HALF), f32)],
        compiler_params=params,
        cost_estimate=pl.CostEstimate(flops=10**9, bytes_accessed=4 * 10**6, transcendentals=0),
    )(data, short_weights, skip, points, strip, turn, spec)
    answer = pl.pallas_call(
        merge_kernel,
        out_shape=like((FILTERS * ROWS, HALF)),
        in_specs=[vmem] * 2,
        out_specs=vmem,
        compiler_params=params,
    )(answer, corr)
    answer = lax.all_to_all(
        answer.reshape(FILTERS, 1, ROWS * HALF),
        "seq",
        split_axis=0,
        concat_axis=0,
        tiled=True,
        axis_index_groups=PARTNERS,
    ).reshape(FILTERS * ROWS, HALF)
    grads, skip_grad, short_grad, filter_grad = pl.pallas_call(
        place_kernel,
        out_shape=(
            like((3, FILTERS, SPAN)),
            like((1, FILTERS)),
            like((3, TAPS, FILTERS)),
            like((4, SPAN)),
        ),
        in_specs=[vmem],
        out_specs=(vmem,) * 4,
        scratch_shapes=[pltpu.VMEM((FILTERS, HALF), f32)],
        compiler_params=params,
    )(answer)
    return grads, filter_grad, skip_grad.reshape(FILTERS), short_grad


def solution(mesh):
    placed = (
        P(None, "chan", "seq"),
        P(None, None, "chan"),
        P(None, "seq"),
        P("chan"),
        P("chan", "seq"),
    )
    return jax.shard_map(
        body,
        mesh=mesh,
        in_specs=placed,
        out_specs=(P(None, "chan", "seq"), P("chan", "seq"), P("chan"), P(None, None, "chan")),
        check_vma=False,
    )
```

```python
import math

import jax
import jax.numpy as jnp
import numpy as np
from jax import lax
from jax.experimental import pallas as pl
from jax.experimental.pallas import tpu as pltpu
from jax.sharding import PartitionSpec as P

f32 = jnp.float32
bf16 = jnp.bfloat16
BLOCKS = 64
SPAN = 256
HALF = 128
FILTERS = 32
GROUPS = 8
TAPS = 3
ROWS = 9
RUN = 8
PARTNERS = [[16 * x + RUN * b + z for x in range(4) for z in range(RUN)] for b in range(2)]


TOTAL = BLOCKS * SPAN


def is_far(g, owner):
    here, there = g // 2, owner // 2
    apart = abs(here - there)
    return (apart == 3) | ((apart == 2) & ((here == 1) | (here == 2)))


def owner_route():
    route = []
    for place in range(BLOCKS):
        for g in range(GROUPS):
            owner = place % RUN ^ g
            target = place ^ RUN if is_far(g, owner) else place
            route.append((place * GROUPS + g, target * GROUPS + owner))
    return route


def split_table(values):
    high = values.astype(jnp.bfloat16)
    low = (values - high.astype(np.float64)).astype(jnp.bfloat16)
    return high, low


def tables():
    rows = np.arange(BLOCKS)
    cols = np.arange(SPAN)
    odd = 4 * rows + 1
    outer = 2 * math.pi * (odd[:, None] * rows[None, :] % 256) / 256.0
    g = np.concatenate([np.cos(outer), -np.sin(outer)], axis=0)
    g_high, g_low = split_table(g)
    forward_rows = np.concatenate([g_high, g_high, g_low], axis=1)
    t = g.T / TOTAL
    t_high, t_low = split_table(t)
    inverse_rows = np.concatenate([t_high, t_low], axis=1)
    near = np.arange(HALF)
    inner = 2 * math.pi * (near[:, None] * near[None, :] % HALF) / HALF
    f = np.concatenate([np.cos(inner), np.sin(inner)], axis=1)
    f_high, f_low = split_table(f)
    points = np.concatenate([f_high, f_high, f_low], axis=0)
    strip = np.zeros((3 * BLOCKS, SPAN), dtype=jnp.bfloat16)
    strip[: 2 * BLOCKS, : 3 * BLOCKS] = forward_rows
    strip[2 * BLOCKS :] = inverse_rows
    full = 2 * math.pi * (odd[:, None] * cols[None, :]) / (4.0 * TOTAL)
    step = 2 * math.pi * near / SPAN
    step = np.concatenate([np.cos(step), np.sin(step)])[None, :] * np.ones((8, 1))
    turn = np.concatenate([np.cos(full), np.sin(full), step]).astype(np.float32)
    return points, strip, turn


def halves(x):
    high = x.astype(bf16)
    return high, (x - high.astype(f32)).astype(bf16)


def place_of(i):
    return i % 4, slice(i // 4 * HALF, (i // 4 + 1) * HALF)


def dot(a, b):
    return jnp.dot(a, b, preferred_element_type=f32)


def dot_left(table, x):
    high, low = halves(x)
    return dot(table, jnp.concatenate([high, low, high], axis=0))


def dot_right(x, table):
    high, low = halves(x)
    return dot(jnp.concatenate([high, low, high], axis=1), table)


def later(x, n):
    row = lax.broadcasted_iota(jnp.int32, x.shape, 0)
    col = lax.broadcasted_iota(jnp.int32, x.shape, 1)
    here = pltpu.roll(x, n, 1)
    above = jnp.where(row == 0, 0.0, pltpu.roll(here, 1, 0))
    return jnp.where(col < n, above, here)


def sooner(x, n):
    row = lax.broadcasted_iota(jnp.int32, x.shape, 0)
    col = lax.broadcasted_iota(jnp.int32, x.shape, 1)
    here = pltpu.roll(x, SPAN - n, 1)
    below = jnp.where(row == BLOCKS - 1, 0.0, pltpu.roll(here, BLOCKS - 1, 0))
    return jnp.where(col >= SPAN - n, below, here)


def pack_kernel(inputs_hbm, grad_hbm, filters_hbm, out_ref, inputs_ref, grad_ref, filters_ref, rows_ref, short_ref, sems):
    copies = [
        pltpu.make_async_copy(source, target, sems.at[i])
        for i, (source, target) in enumerate(
            [(inputs_hbm, inputs_ref), (grad_hbm, grad_ref), (filters_hbm, filters_ref)]
        )
    ]
    for copy in copies:
        copy.start()
    for copy in copies:
        copy.wait()
    h = filters_ref[...]
    h_high = h.astype(bf16).astype(f32)
    parts = [inputs_ref[b].astype(f32) for b in range(3)]
    parts += [grad_ref[...].astype(f32), h_high, h - h_high]
    for i, part in enumerate(parts):
        for side in range(2):
            row, tile = place_of(2 * i + side)
            rows_ref[:, row, tile] = part[:, side * HALF : (side + 1) * HALF]
    short_ref[...] = rows_ref[...].astype(bf16)
    g = lax.axis_index("chan")
    for place in range(BLOCKS):
        out_ref[place] = short_ref[4 * jnp.bitwise_xor(g, place % RUN) + place // (2 * RUN)]


def whole_sum(x):
    return jnp.sum(jnp.sum(x, axis=0, keepdims=True), axis=1, keepdims=True)


def seat():
    place, g = lax.axis_index("seq"), lax.axis_index("chan")
    owner = jnp.bitwise_xor(lax.rem(place, RUN), g)
    return g, owner, 4 * owner + place // (2 * RUN), lax.rem(place // RUN, 2)


def own_taps(taps_ref, channel):
    lane = lax.broadcasted_iota(jnp.int32, taps_ref.shape, 2)
    own = jnp.sum(jnp.where(lane == channel, taps_ref[...], 0.0), axis=2, keepdims=True)
    return [[own[b, j : j + 1, :] for j in range(TAPS)] for b in range(3)]


def unpack(data_ref, rows_ref, count):
    width = count // 2 * HALF
    rows_ref[:, :, :width] = data_ref[:, :, :width].astype(f32)
    parts = []
    for i in range(count):
        pieces = []
        for side in range(2):
            row, tile = place_of(2 * i + side)
            pieces.append(rows_ref[:, row, tile])
        parts.append(jnp.concatenate(pieces, axis=1))
    return parts


def mix(branch, taps):
    moved = [[x] + [later(x, j) for j in range(1, TAPS)] for x in branch]
    mixed = [
        taps[b][0] * moved[b][0] + taps[b][1] * moved[b][1] + taps[b][2] * moved[b][2]
        for b in range(3)
    ]
    return moved, mixed


def constants(strip_ref, turn_ref):
    left = strip_ref[: 2 * BLOCKS, : 3 * BLOCKS]
    right = strip_ref[2 * BLOCKS :, :]
    right = jnp.concatenate([right[:, :HALF], right], axis=1)
    last = 2 * BLOCKS
    odd = turn_ref[last : last + 1, :HALF], turn_ref[last : last + 1, HALF:]
    return left, right, (turn_ref[:BLOCKS, :], turn_ref[BLOCKS:last, :]), odd


def pair(values, i):
    re = values[2 * i * BLOCKS : (2 * i + 1) * BLOCKS]
    im = values[(2 * i + 1) * BLOCKS : (2 * i + 2) * BLOCKS]
    return re[:, :HALF], re[:, HALF:], im[:, :HALF], im[:, HALF:]


def spectra(signals, points, left, turn, odd):
    cosine, sine = turn
    odd_cos, odd_sin = odd
    start = dot_left(left, jnp.concatenate(signals, axis=1))
    stacked = []
    for i in range(len(signals)):
        re = start[:BLOCKS, i * SPAN : (i + 1) * SPAN]
        im = start[BLOCKS:, i * SPAN : (i + 1) * SPAN]
        re, im = re * cosine + im * sine, im * cosine - re * sine
        stacked += [re[:, :HALF] + re[:, HALF:], im[:, :HALF] + im[:, HALF:]]
        re, im = re[:, :HALF] - re[:, HALF:], im[:, :HALF] - im[:, HALF:]
        stacked += [re * odd_cos + im * odd_sin, im * odd_cos - re * odd_sin]
    values = dot_right(jnp.concatenate(stacked, axis=0), points)
    results = []
    for i in range(2 * len(signals)):
        re_cos, re_sin, im_cos, im_sin = pair(values, i)
        results.append((re_cos + im_sin, im_cos - re_sin))
    return [results[2 * i : 2 * i + 2] for i in range(len(signals))]


def times(a, b):
    return a[0] * b[0] - a[1] * b[1], a[0] * b[1] + a[1] * b[0]


def times_conj(a, b):
    return a[0] * b[0] + a[1] * b[1], a[1] * b[0] - a[0] * b[1]


def inverse(spectrums, points, right, turn, odd):
    cosine, sine = turn
    odd_cos, odd_sin = odd
    joined = [x for spectrum in spectrums for part in spectrum for x in part]
    back = dot_right(jnp.concatenate(joined, axis=0), points)
    turned = []
    for i in range(len(spectrums)):
        re_cos, re_sin, im_cos, im_sin = pair(back, 2 * i)
        even_re, even_im = re_cos - im_sin, im_cos + re_sin
        re_cos, re_sin, im_cos, im_sin = pair(back, 2 * i + 1)
        re, im = re_cos - im_sin, im_cos + re_sin
        re, im = re * odd_cos - im * odd_sin, im * odd_cos + re * odd_sin
        b_re = jnp.concatenate([even_re + re, even_re - re], axis=1)
        b_im = jnp.concatenate([even_im + im, even_im - im], axis=1)
        turned.append(
            jnp.concatenate([b_re * cosine - b_im * sine, b_im * cosine + b_re * sine], axis=0)
        )
    return dot_left(right, jnp.concatenate(turned, axis=1))


def every_second_run(x, b):
    runs = [
        jnp.where(b == 0, x[first : first + RUN], x[first + RUN : first + 2 * RUN])
        for first in range(0, BLOCKS, 2 * RUN)
    ]
    return jnp.concatenate(runs, axis=0)


def corr_kernel(
    data_ref, taps_ref, skip_ref, points_ref, strip_ref, turn_ref, corr_ref, spec_ref, rows_ref
):
    g, owner, channel, b_own = seat()
    parts = unpack(data_ref, rows_ref, 4)
    taps = own_taps(taps_ref, channel)
    _, (query, key, value) = mix(parts[:3], taps)
    product, dw = key * value, parts[3] * query
    left, right, turn, odd = constants(strip_ref, turn_ref)
    points = points_ref[...]
    p, d = spectra([product, dw], points, left, turn, odd)
    for i, x in enumerate([x for spectrum in (p, d) for part in spectrum for x in part]):
        spec_ref[i * BLOCKS : (i + 1) * BLOCKS, :] = x
    corr = inverse([[times_conj(d[e], p[e]) for e in range(2)]], points, right, turn, odd)
    b_there = jnp.where(is_far(g, owner), 1 - b_own, b_own)
    corr = every_second_run(corr, b_there)
    for side in range(2):
        corr_ref[side * FILTERS : (side + 1) * FILTERS, :] = corr[:, side * HALF : (side + 1) * HALF]


def channel_kernel(
    data_ref, taps_ref, skip_ref, points_ref, strip_ref, turn_ref, spec_ref, out_ref, rows_ref
):
    _, _, channel, b_own = seat()
    parts = unpack(data_ref, rows_ref, 6)
    grad, h = parts[3], parts[4] + parts[5]
    taps = own_taps(taps_ref, channel)
    lane = lax.broadcasted_iota(jnp.int32, (1, FILTERS), 1)
    line = skip_ref[...].reshape(1, FILTERS)
    direct = jnp.sum(jnp.where(lane == channel, line, 0.0), axis=1, keepdims=True)
    moved, (query, key, value) = mix(parts[:3], taps)
    product, dw = key * value, grad * query
    left, right, turn, odd = constants(strip_ref, turn_ref)
    points = points_ref[...]
    (h_spec,) = spectra([h], points, left, turn, odd)
    held = [spec_ref[i * BLOCKS : (i + 1) * BLOCKS, :] for i in range(8)]
    p = [(held[0], held[1]), (held[2], held[3])]
    d = [(held[4], held[5]), (held[6], held[7])]
    result = inverse(
        [
            [times(h_spec[e], p[e]) for e in range(2)],
            [times_conj(d[e], h_spec[e]) for e in range(2)],
        ],
        points,
        right,
        turn,
        odd,
    )
    conv_out = result[:, :SPAN] + direct * product
    dz = result[:, SPAN:] + direct * dw

    grads = [grad * conv_out, dz * value, dz * key]
    for b in range(3):
        g = grads[b]
        total = taps[b][0] * g + taps[b][1] * sooner(g, 1) + taps[b][2] * sooner(g, 2)
        mine = every_second_run(total, b_own)
        for side in range(2):
            out_ref[pl.ds(2 * b + side, FILTERS, stride=ROWS), :] = mine[
                :, side * HALF : (side + 1) * HALF
            ]
    for row in (6, 7):
        out_ref[pl.ds(row, FILTERS, stride=ROWS), :] = jnp.zeros((FILTERS, HALF), f32)
    sums = [whole_sum(grads[b] * moved[b][j]) for b in range(3) for j in range(TAPS)]
    sums.append(whole_sum(dw * product))
    lanes = lax.broadcasted_iota(jnp.int32, (1, HALF), 1)
    line = jnp.zeros((1, HALF), f32)
    for i, value in enumerate(sums):
        line = jnp.where(lanes == i, value, line)
    line = jnp.broadcast_to(line * TOTAL**-0.5, (FILTERS, HALF))
    out_ref[pl.ds(8, FILTERS, stride=ROWS), :] = line


def merge_kernel(answer_ref, corr_ref, out_ref):
    out_ref[...] = answer_ref[...]
    for side in range(2):
        out_ref[pl.ds(6 + side, FILTERS, stride=ROWS), :] = corr_ref[
            side * FILTERS : (side + 1) * FILTERS, :
        ]


def place_kernel(data_ref, grads_ref, skip_ref, short_ref, filter_ref, sums_ref):
    g = lax.axis_index("chan")
    for owner in range(GROUPS):
        first = ROWS * jnp.bitwise_xor(g, owner)
        rows = slice(4 * owner, 4 * owner + 4)
        for b in range(3):
            for side in range(2):
                grads_ref[b, rows, side * HALF : (side + 1) * HALF] = data_ref[
                    pl.ds(first + (2 * b + side), 4, stride=RUN * ROWS), :
                ]
        sums_ref[rows, :] = data_ref[pl.ds(first + 8, 4, stride=RUN * ROWS), :]
    padded = jnp.concatenate([sums_ref[...], jnp.zeros((HALF - FILTERS, HALF), f32)], axis=0)
    flipped = padded.T[:, :FILTERS]
    for b in range(3):
        short_ref[b] = flipped[TAPS * b : TAPS * (b + 1), :]
    skip_ref[...] = flipped[9:10, :]
    for x in range(4):
        for side in range(2):
            terms = data_ref[pl.ds(x * RUN * ROWS + 6 + side, RUN, stride=ROWS), :]
            total = jnp.sum(terms, axis=0, keepdims=True) * (TOTAL * GROUPS) ** -0.5
            filter_ref[x : x + 1, side * HALF : (side + 1) * HALF] = total


vmem = pl.BlockSpec(memory_space=pltpu.VMEM)
hbm = pl.BlockSpec(memory_space=pltpu.HBM)
params = pltpu.CompilerParams(vmem_limit_bytes=32 * 1024 * 1024)


def like(shape, dtype=f32):
    return jax.ShapeDtypeStruct(shape, dtype)


def body(inputs, short_weights, filters, skip, grad_out):
    points, strip, turn = [jnp.asarray(values) for values in tables()]
    message = pl.pallas_call(
        pack_kernel,
        out_shape=like((BLOCKS, 4, 3 * HALF), bf16),
        in_specs=[hbm] * 3,
        out_specs=vmem,
        scratch_shapes=[
            pltpu.VMEM((3, FILTERS, SPAN), bf16),
            pltpu.VMEM((FILTERS, SPAN), bf16),
            pltpu.VMEM((FILTERS, SPAN), f32),
            pltpu.VMEM((FILTERS, 4, 3 * HALF), f32),
            pltpu.VMEM((FILTERS, 4, 3 * HALF), bf16),
            pltpu.SemaphoreType.DMA((3,)),
        ],
        compiler_params=params,
    )(*[pltpu.with_memory_space_constraint(x, pltpu.HBM) for x in (inputs, grad_out, filters)])
    data = lax.all_to_all(message, "seq", split_axis=0, concat_axis=0, tiled=True)
    corr, spec = pl.pallas_call(
        corr_kernel,
        out_shape=(like((BLOCKS, HALF)), like((8 * BLOCKS, HALF))),
        in_specs=[vmem] * 6,
        out_specs=(vmem,) * 2,
        scratch_shapes=[pltpu.VMEM((BLOCKS, 4, 3 * HALF), f32)],
        compiler_params=params,
    )(data, short_weights, skip, points, strip, turn)
    corr = lax.ppermute(corr, ("seq", "chan"), owner_route())
    answer = pl.pallas_call(
        channel_kernel,
        out_shape=like((FILTERS * ROWS, HALF)),
        in_specs=[vmem] * 7,
        out_specs=vmem,
        scratch_shapes=[pltpu.VMEM((BLOCKS, 4, 3 * HALF), f32)],
        compiler_params=params,
        cost_estimate=pl.CostEstimate(flops=10**9, bytes_accessed=4 * 10**6, transcendentals=0),
    )(data, short_weights, skip, points, strip, turn, spec)
    answer = pl.pallas_call(
        merge_kernel,
        out_shape=like((FILTERS * ROWS, HALF)),
        in_specs=[vmem] * 2,
        out_specs=vmem,
        compiler_params=params,
    )(answer, corr)
    answer = lax.all_to_all(
        answer.reshape(FILTERS, 1, ROWS * HALF),
        "seq",
        split_axis=0,
        concat_axis=0,
        tiled=True,
        axis_index_groups=PARTNERS,
    ).reshape(FILTERS * ROWS, HALF)
    grads, skip_grad, short_grad, filter_grad = pl.pallas_call(
        place_kernel,
        out_shape=(
            like((3, FILTERS, SPAN)),
            like((1, FILTERS)),
            like((3, TAPS, FILTERS)),
            like((4, SPAN)),
        ),
        in_specs=[vmem],
        out_specs=(vmem,) * 4,
        scratch_shapes=[pltpu.VMEM((FILTERS, HALF), f32)],
        compiler_params=params,
    )(answer)
    return grads, filter_grad, skip_grad.reshape(FILTERS), short_grad


def solution(mesh):
    placed = (
        P(None, "chan", "seq"),
        P(None, None, "chan"),
        P(None, "seq"),
        P("chan"),
        P("chan", "seq"),
    )
    return jax.shard_map(
        body,
        mesh=mesh,
        in_specs=placed,
        out_specs=(P(None, "chan", "seq"), P("chan", "seq"), P("chan"), P(None, None, "chan")),
        check_vma=False,
    )
```

```python
import math

import jax
import jax.numpy as jnp
import numpy as np
from jax import lax
from jax.experimental import pallas as pl
from jax.experimental.pallas import tpu as pltpu
from jax.sharding import PartitionSpec as P

f32 = jnp.float32
bf16 = jnp.bfloat16
BLOCKS = 64
SPAN = 256
HALF = 128
FILTERS = 32
GROUPS = 8
TAPS = 3
ROWS = 9
RUN = 8
PARTNERS = [[16 * x + RUN * b + z for x in range(4) for z in range(RUN)] for b in range(2)]


TOTAL = BLOCKS * SPAN


def is_far(g, owner):
    return abs(g // 2 - owner // 2) == 3


def owner_route():
    route = []
    for place in range(BLOCKS):
        for g in range(GROUPS):
            owner = place % RUN ^ g
            target = place ^ RUN if is_far(g, owner) else place
            route.append((place * GROUPS + g, target * GROUPS + owner))
    return route


def split_table(values):
    high = values.astype(jnp.bfloat16)
    low = (values - high.astype(np.float64)).astype(jnp.bfloat16)
    return high, low


def tables():
    rows = np.arange(BLOCKS)
    cols = np.arange(SPAN)
    odd = 4 * rows + 1
    outer = 2 * math.pi * (odd[:, None] * rows[None, :] % 256) / 256.0
    g = np.concatenate([np.cos(outer), -np.sin(outer)], axis=0)
    g_high, g_low = split_table(g)
    forward_rows = np.concatenate([g_high, g_high, g_low], axis=1)
    t = g.T / TOTAL
    t_high, t_low = split_table(t)
    inverse_rows = np.concatenate([t_high, t_low], axis=1)
    near = np.arange(HALF)
    inner = 2 * math.pi * (near[:, None] * near[None, :] % HALF) / HALF
    f = np.concatenate([np.cos(inner), np.sin(inner)], axis=1)
    f_high, f_low = split_table(f)
    points = np.concatenate([f_high, f_high, f_low], axis=0)
    strip = np.zeros((3 * BLOCKS, SPAN), dtype=jnp.bfloat16)
    strip[: 2 * BLOCKS, : 3 * BLOCKS] = forward_rows
    strip[2 * BLOCKS :] = inverse_rows
    full = 2 * math.pi * (odd[:, None] * cols[None, :]) / (4.0 * TOTAL)
    step = 2 * math.pi * near / SPAN
    step = np.concatenate([np.cos(step), np.sin(step)])[None, :] * np.ones((8, 1))
    turn = np.concatenate([np.cos(full), np.sin(full), step]).astype(np.float32)
    return points, strip, turn


def halves(x):
    high = x.astype(bf16)
    return high, (x - high.astype(f32)).astype(bf16)


def place_of(i):
    return i % 4, slice(i // 4 * HALF, (i // 4 + 1) * HALF)


def dot(a, b):
    return jnp.dot(a, b, preferred_element_type=f32)


def dot_left(table, x):
    high, low = halves(x)
    return dot(table, jnp.concatenate([high, low, high], axis=0))


def dot_right(x, table):
    high, low = halves(x)
    wide = jnp.concatenate([high, low], axis=1)
    return dot(wide, table[: 2 * HALF]) + dot(high, table[2 * HALF :])


def later(x, n):
    row = lax.broadcasted_iota(jnp.int32, x.shape, 0)
    col = lax.broadcasted_iota(jnp.int32, x.shape, 1)
    here = pltpu.roll(x, n, 1)
    above = jnp.where(row == 0, 0.0, pltpu.roll(here, 1, 0))
    return jnp.where(col < n, above, here)


def sooner(x, n):
    row = lax.broadcasted_iota(jnp.int32, x.shape, 0)
    col = lax.broadcasted_iota(jnp.int32, x.shape, 1)
    here = pltpu.roll(x, SPAN - n, 1)
    below = jnp.where(row == BLOCKS - 1, 0.0, pltpu.roll(here, BLOCKS - 1, 0))
    return jnp.where(col >= SPAN - n, below, here)


def pack_kernel(inputs_hbm, grad_hbm, filters_hbm, out_ref, inputs_ref, grad_ref, filters_ref, rows_ref, short_ref, sems):
    copies = [
        pltpu.make_async_copy(source, target, sems.at[i])
        for i, (source, target) in enumerate(
            [(inputs_hbm, inputs_ref), (grad_hbm, grad_ref), (filters_hbm, filters_ref)]
        )
    ]
    for copy in copies:
        copy.start()

    def put(i, part):
        for side in range(2):
            row, tile = place_of(2 * i + side)
            rows_ref[:, row, tile] = part[:, side * HALF : (side + 1) * HALF]

    copies[2].wait()
    h = filters_ref[...]
    h_high = h.astype(bf16).astype(f32)
    put(4, h_high)
    put(5, h - h_high)
    copies[1].wait()
    put(3, grad_ref[...].astype(f32))
    short_ref[:, :, 2 * HALF :] = rows_ref[:, :, 2 * HALF :].astype(bf16)
    copies[0].wait()
    for b in range(3):
        put(b, inputs_ref[b].astype(f32))
    short_ref[:, :, : 2 * HALF] = rows_ref[:, :, : 2 * HALF].astype(bf16)
    g = lax.axis_index("chan")
    for place in range(BLOCKS):
        out_ref[place] = short_ref[4 * jnp.bitwise_xor(g, place % RUN) + place // (2 * RUN)]


def whole_sum(x):
    return jnp.sum(jnp.sum(x, axis=0, keepdims=True), axis=1, keepdims=True)


def seat():
    place, g = lax.axis_index("seq"), lax.axis_index("chan")
    owner = jnp.bitwise_xor(lax.rem(place, RUN), g)
    return g, owner, 4 * owner + place // (2 * RUN), lax.rem(place // RUN, 2)


def own_taps(taps_ref, channel):
    lane = lax.broadcasted_iota(jnp.int32, taps_ref.shape, 2)
    own = jnp.sum(jnp.where(lane == channel, taps_ref[...], 0.0), axis=2, keepdims=True)
    return [[own[b, j : j + 1, :] for j in range(TAPS)] for b in range(3)]


def unpack(data_ref, rows_ref, count):
    width = count // 2 * HALF
    rows_ref[:, :, :width] = data_ref[:, :, :width].astype(f32)
    parts = []
    for i in range(count):
        pieces = []
        for side in range(2):
            row, tile = place_of(2 * i + side)
            pieces.append(rows_ref[:, row, tile])
        parts.append(jnp.concatenate(pieces, axis=1))
    return parts


def mix(branch, taps):
    moved = [[x] + [later(x, j) for j in range(1, TAPS)] for x in branch]
    mixed = [
        taps[b][0] * moved[b][0] + taps[b][1] * moved[b][1] + taps[b][2] * moved[b][2]
        for b in range(3)
    ]
    return moved, mixed


def constants(strip_ref, turn_ref):
    left = strip_ref[: 2 * BLOCKS, : 3 * BLOCKS]
    right = strip_ref[2 * BLOCKS :, :]
    right = jnp.concatenate([right[:, :HALF], right], axis=1)
    last = 2 * BLOCKS
    odd = turn_ref[last : last + 1, :HALF], turn_ref[last : last + 1, HALF:]
    return left, right, (turn_ref[:BLOCKS, :], turn_ref[BLOCKS:last, :]), odd


def pair(values, i):
    re = values[2 * i * BLOCKS : (2 * i + 1) * BLOCKS]
    im = values[(2 * i + 1) * BLOCKS : (2 * i + 2) * BLOCKS]
    return re[:, :HALF], re[:, HALF:], im[:, :HALF], im[:, HALF:]


def spectra(signals, points, left, turn, odd):
    cosine, sine = turn
    odd_cos, odd_sin = odd
    start = dot_left(left, jnp.concatenate(signals, axis=1))
    stacked = []
    for i in range(len(signals)):
        re = start[:BLOCKS, i * SPAN : (i + 1) * SPAN]
        im = start[BLOCKS:, i * SPAN : (i + 1) * SPAN]
        re, im = re * cosine + im * sine, im * cosine - re * sine
        stacked += [re[:, :HALF] + re[:, HALF:], im[:, :HALF] + im[:, HALF:]]
        re, im = re[:, :HALF] - re[:, HALF:], im[:, :HALF] - im[:, HALF:]
        stacked += [re * odd_cos + im * odd_sin, im * odd_cos - re * odd_sin]
    values = dot_right(jnp.concatenate(stacked, axis=0), points)
    results = []
    for i in range(2 * len(signals)):
        re_cos, re_sin, im_cos, im_sin = pair(values, i)
        results.append((re_cos + im_sin, im_cos - re_sin))
    return [results[2 * i : 2 * i + 2] for i in range(len(signals))]


def times(a, b):
    return a[0] * b[0] - a[1] * b[1], a[0] * b[1] + a[1] * b[0]


def times_conj(a, b):
    return a[0] * b[0] + a[1] * b[1], a[1] * b[0] - a[0] * b[1]


def inverse(spectrums, points, right, turn, odd):
    cosine, sine = turn
    odd_cos, odd_sin = odd
    joined = [x for spectrum in spectrums for part in spectrum for x in part]
    back = dot_right(jnp.concatenate(joined, axis=0), points)
    turned = []
    for i in range(len(spectrums)):
        re_cos, re_sin, im_cos, im_sin = pair(back, 2 * i)
        even_re, even_im = re_cos - im_sin, im_cos + re_sin
        re_cos, re_sin, im_cos, im_sin = pair(back, 2 * i + 1)
        re, im = re_cos - im_sin, im_cos + re_sin
        re, im = re * odd_cos - im * odd_sin, im * odd_cos + re * odd_sin
        b_re = jnp.concatenate([even_re + re, even_re - re], axis=1)
        b_im = jnp.concatenate([even_im + im, even_im - im], axis=1)
        turned.append(
            jnp.concatenate([b_re * cosine - b_im * sine, b_im * cosine + b_re * sine], axis=0)
        )
    return dot_left(right, jnp.concatenate(turned, axis=1))


def every_second_run(x, b):
    runs = [
        jnp.where(b == 0, x[first : first + RUN], x[first + RUN : first + 2 * RUN])
        for first in range(0, BLOCKS, 2 * RUN)
    ]
    return jnp.concatenate(runs, axis=0)


def corr_kernel(
    data_ref, taps_ref, skip_ref, points_ref, strip_ref, turn_ref, corr_ref, spec_ref, rows_ref
):
    g, owner, channel, b_own = seat()
    parts = unpack(data_ref, rows_ref, 4)
    taps = own_taps(taps_ref, channel)
    _, (query, key, value) = mix(parts[:3], taps)
    product, dw = key * value, parts[3] * query
    left, right, turn, odd = constants(strip_ref, turn_ref)
    points = points_ref[...]
    p, d = spectra([product, dw], points, left, turn, odd)
    for i, x in enumerate([x for spectrum in (p, d) for part in spectrum for x in part]):
        spec_ref[i * BLOCKS : (i + 1) * BLOCKS, :] = x
    corr = inverse([[times_conj(d[e], p[e]) for e in range(2)]], points, right, turn, odd)
    b_there = jnp.where(is_far(g, owner), 1 - b_own, b_own)
    corr = every_second_run(corr, b_there)
    for side in range(2):
        corr_ref[side * FILTERS : (side + 1) * FILTERS, :] = corr[:, side * HALF : (side + 1) * HALF]


def channel_kernel(
    data_ref, taps_ref, skip_ref, points_ref, strip_ref, turn_ref, spec_ref, out_ref, rows_ref
):
    _, _, channel, b_own = seat()
    parts = unpack(data_ref, rows_ref, 6)
    grad, h = parts[3], parts[4] + parts[5]
    taps = own_taps(taps_ref, channel)
    lane = lax.broadcasted_iota(jnp.int32, (1, FILTERS), 1)
    line = skip_ref[...].reshape(1, FILTERS)
    direct = jnp.sum(jnp.where(lane == channel, line, 0.0), axis=1, keepdims=True)
    moved, (query, key, value) = mix(parts[:3], taps)
    product, dw = key * value, grad * query
    left, right, turn, odd = constants(strip_ref, turn_ref)
    points = points_ref[...]
    (h_spec,) = spectra([h], points, left, turn, odd)
    held = [spec_ref[i * BLOCKS : (i + 1) * BLOCKS, :] for i in range(8)]
    p = [(held[0], held[1]), (held[2], held[3])]
    d = [(held[4], held[5]), (held[6], held[7])]
    result = inverse(
        [
            [times(h_spec[e], p[e]) for e in range(2)],
            [times_conj(d[e], h_spec[e]) for e in range(2)],
        ],
        points,
        right,
        turn,
        odd,
    )
    conv_out = result[:, :SPAN] + direct * product
    dz = result[:, SPAN:] + direct * dw

    grads = [grad * conv_out, dz * value, dz * key]
    for b in range(3):
        g = grads[b]
        total = taps[b][0] * g + taps[b][1] * sooner(g, 1) + taps[b][2] * sooner(g, 2)
        mine = every_second_run(total, b_own)
        for side in range(2):
            out_ref[pl.ds(2 * b + side, FILTERS, stride=ROWS), :] = mine[
                :, side * HALF : (side + 1) * HALF
            ]
    for row in (6, 7):
        out_ref[pl.ds(row, FILTERS, stride=ROWS), :] = jnp.zeros((FILTERS, HALF), f32)
    sums = [whole_sum(grads[b] * moved[b][j]) for b in range(3) for j in range(TAPS)]
    sums.append(whole_sum(dw * product))
    lanes = lax.broadcasted_iota(jnp.int32, (1, HALF), 1)
    line = jnp.zeros((1, HALF), f32)
    for i, value in enumerate(sums):
        line = jnp.where(lanes == i, value, line)
    line = jnp.broadcast_to(line * TOTAL**-0.5, (FILTERS, HALF))
    out_ref[pl.ds(8, FILTERS, stride=ROWS), :] = line


def merge_kernel(answer_ref, corr_ref, out_ref):
    out_ref[...] = answer_ref[...]
    for side in range(2):
        out_ref[pl.ds(6 + side, FILTERS, stride=ROWS), :] = corr_ref[
            side * FILTERS : (side + 1) * FILTERS, :
        ]


def place_kernel(data_ref, grads_ref, skip_ref, short_ref, filter_ref, sums_ref):
    g = lax.axis_index("chan")
    for owner in range(GROUPS):
        first = ROWS * jnp.bitwise_xor(g, owner)
        rows = slice(4 * owner, 4 * owner + 4)
        for b in range(3):
            for side in range(2):
                grads_ref[b, rows, side * HALF : (side + 1) * HALF] = data_ref[
                    pl.ds(first + (2 * b + side), 4, stride=RUN * ROWS), :
                ]
        sums_ref[rows, :] = data_ref[pl.ds(first + 8, 4, stride=RUN * ROWS), :]
    padded = jnp.concatenate([sums_ref[...], jnp.zeros((HALF - FILTERS, HALF), f32)], axis=0)
    flipped = padded.T[:, :FILTERS]
    for b in range(3):
        short_ref[b] = flipped[TAPS * b : TAPS * (b + 1), :]
    skip_ref[...] = flipped[9:10, :]
    for x in range(4):
        for side in range(2):
            terms = data_ref[pl.ds(x * RUN * ROWS + 6 + side, RUN, stride=ROWS), :]
            total = jnp.sum(terms, axis=0, keepdims=True) * (TOTAL * GROUPS) ** -0.5
            filter_ref[x : x + 1, side * HALF : (side + 1) * HALF] = total


vmem = pl.BlockSpec(memory_space=pltpu.VMEM)
hbm = pl.BlockSpec(memory_space=pltpu.HBM)
params = pltpu.CompilerParams(vmem_limit_bytes=32 * 1024 * 1024)


def like(shape, dtype=f32):
    return jax.ShapeDtypeStruct(shape, dtype)


def body(inputs, short_weights, filters, skip, grad_out):
    points, strip, turn = [jnp.asarray(values) for values in tables()]
    message = pl.pallas_call(
        pack_kernel,
        out_shape=like((BLOCKS, 4, 3 * HALF), bf16),
        in_specs=[hbm] * 3,
        out_specs=vmem,
        scratch_shapes=[
            pltpu.VMEM((3, FILTERS, SPAN), bf16),
            pltpu.VMEM((FILTERS, SPAN), bf16),
            pltpu.VMEM((FILTERS, SPAN), f32),
            pltpu.VMEM((FILTERS, 4, 3 * HALF), f32),
            pltpu.VMEM((FILTERS, 4, 3 * HALF), bf16),
            pltpu.SemaphoreType.DMA((3,)),
        ],
        compiler_params=params,
    )(*[pltpu.with_memory_space_constraint(x, pltpu.HBM) for x in (inputs, grad_out, filters)])
    data = lax.all_to_all(message, "seq", split_axis=0, concat_axis=0, tiled=True)
    corr, spec = pl.pallas_call(
        corr_kernel,
        out_shape=(like((BLOCKS, HALF)), like((8 * BLOCKS, HALF))),
        in_specs=[vmem] * 6,
        out_specs=(vmem,) * 2,
        scratch_shapes=[pltpu.VMEM((BLOCKS, 4, 3 * HALF), f32)],
        compiler_params=params,
    )(data, short_weights, skip, points, strip, turn)
    corr = lax.ppermute(corr, ("seq", "chan"), owner_route())
    answer = pl.pallas_call(
        channel_kernel,
        out_shape=like((FILTERS * ROWS, HALF)),
        in_specs=[vmem] * 7,
        out_specs=vmem,
        scratch_shapes=[pltpu.VMEM((BLOCKS, 4, 3 * HALF), f32)],
        compiler_params=params,
        cost_estimate=pl.CostEstimate(flops=10**9, bytes_accessed=4 * 10**6, transcendentals=0),
    )(data, short_weights, skip, points, strip, turn, spec)
    answer = pl.pallas_call(
        merge_kernel,
        out_shape=like((FILTERS * ROWS, HALF)),
        in_specs=[vmem] * 2,
        out_specs=vmem,
        compiler_params=params,
    )(answer, corr)
    answer = lax.all_to_all(
        answer.reshape(FILTERS, 1, ROWS * HALF),
        "seq",
        split_axis=0,
        concat_axis=0,
        tiled=True,
        axis_index_groups=PARTNERS,
    ).reshape(FILTERS * ROWS, HALF)
    grads, skip_grad, short_grad, filter_grad = pl.pallas_call(
        place_kernel,
        out_shape=(
            like((3, FILTERS, SPAN)),
            like((1, FILTERS)),
            like((3, TAPS, FILTERS)),
            like((4, SPAN)),
        ),
        in_specs=[vmem],
        out_specs=(vmem,) * 4,
        scratch_shapes=[pltpu.VMEM((FILTERS, HALF), f32)],
        compiler_params=params,
    )(answer)
    return grads, filter_grad, skip_grad.reshape(FILTERS), short_grad


def solution(mesh):
    placed = (
        P(None, "chan", "seq"),
        P(None, None, "chan"),
        P(None, "seq"),
        P("chan"),
        P("chan", "seq"),
    )
    return jax.shard_map(
        body,
        mesh=mesh,
        in_specs=placed,
        out_specs=(P(None, "chan", "seq"), P("chan", "seq"), P("chan"), P(None, None, "chan")),
        check_vma=False,
    )
```

```python
import math

import jax
import jax.numpy as jnp
import numpy as np
from jax import lax
from jax.experimental import pallas as pl
from jax.experimental.pallas import tpu as pltpu
from jax.sharding import PartitionSpec as P

f32 = jnp.float32
bf16 = jnp.bfloat16
BLOCKS = 64
SPAN = 256
HALF = 128
FILTERS = 32
GROUPS = 8
TAPS = 3
ROWS = 9
RUN = 8
PARTNERS = [[16 * x + RUN * b + z for x in range(4) for z in range(RUN)] for b in range(2)]


TOTAL = BLOCKS * SPAN


def is_far(g, owner):
    return abs(g // 2 - owner // 2) == 3


def owner_route():
    route = []
    for place in range(BLOCKS):
        for g in range(GROUPS):
            owner = place % RUN ^ g
            target = place ^ RUN if is_far(g, owner) else place
            route.append((place * GROUPS + g, target * GROUPS + owner))
    return route


def split_table(values):
    high = values.astype(jnp.bfloat16)
    low = (values - high.astype(np.float64)).astype(jnp.bfloat16)
    return high, low


def tables():
    rows = np.arange(BLOCKS)
    cols = np.arange(SPAN)
    odd = 4 * rows + 1
    outer = 2 * math.pi * (odd[:, None] * rows[None, :] % 256) / 256.0
    g = np.concatenate([np.cos(outer), -np.sin(outer)], axis=0)
    g_high, g_low = split_table(g)
    forward_rows = np.concatenate([g_high, g_high, g_low], axis=1)
    t = g.T / TOTAL
    t_high, t_low = split_table(t)
    inverse_rows = np.concatenate([t_high, t_low], axis=1)
    near = np.arange(HALF)
    inner = 2 * math.pi * (near[:, None] * near[None, :] % HALF) / HALF
    f = np.concatenate([np.cos(inner), np.sin(inner)], axis=1)
    f_high, f_low = split_table(f)
    points = np.concatenate([f_high, f_high, f_low], axis=0)
    strip = np.zeros((3 * BLOCKS, SPAN), dtype=jnp.bfloat16)
    strip[: 2 * BLOCKS, : 3 * BLOCKS] = forward_rows
    strip[2 * BLOCKS :] = inverse_rows
    full = 2 * math.pi * (odd[:, None] * cols[None, :]) / (4.0 * TOTAL)
    step = 2 * math.pi * near / SPAN
    step = np.concatenate([np.cos(step), np.sin(step)])[None, :] * np.ones((8, 1))
    turn = np.concatenate([np.cos(full), np.sin(full), step]).astype(np.float32)
    return points, strip, turn


def halves(x):
    high = x.astype(bf16)
    return high, (x - high.astype(f32)).astype(bf16)


def place_of(i):
    return i % 4, slice(i // 4 * HALF, (i // 4 + 1) * HALF)


def dot(a, b):
    return jnp.dot(a, b, preferred_element_type=f32)


def dot_left(table, x):
    high, low = halves(x)
    return dot(table, jnp.concatenate([high, low, high], axis=0))


def dot_right(x, table):
    high, low = halves(x)
    return dot(jnp.concatenate([high, low, high], axis=1), table)


def later(x, n):
    row = lax.broadcasted_iota(jnp.int32, x.shape, 0)
    col = lax.broadcasted_iota(jnp.int32, x.shape, 1)
    here = pltpu.roll(x, n, 1)
    above = jnp.where(row == 0, 0.0, pltpu.roll(here, 1, 0))
    return jnp.where(col < n, above, here)


def sooner(x, n):
    row = lax.broadcasted_iota(jnp.int32, x.shape, 0)
    col = lax.broadcasted_iota(jnp.int32, x.shape, 1)
    here = pltpu.roll(x, SPAN - n, 1)
    below = jnp.where(row == BLOCKS - 1, 0.0, pltpu.roll(here, BLOCKS - 1, 0))
    return jnp.where(col >= SPAN - n, below, here)


def pack_kernel(inputs_hbm, grad_hbm, filters_hbm, out_ref, inputs_ref, grad_ref, filters_ref, rows_ref, short_ref, sems):
    copies = [
        pltpu.make_async_copy(source, target, sems.at[i])
        for i, (source, target) in enumerate(
            [(inputs_hbm, inputs_ref), (grad_hbm, grad_ref), (filters_hbm, filters_ref)]
        )
    ]
    for copy in copies:
        copy.start()
    for copy in copies:
        copy.wait()
    h = filters_ref[...]
    h_high = h.astype(bf16).astype(f32)
    parts = [inputs_ref[b].astype(f32) for b in range(3)]
    parts += [grad_ref[...].astype(f32), h_high, h - h_high]
    for i, part in enumerate(parts):
        for side in range(2):
            row, tile = place_of(2 * i + side)
            rows_ref[:, row, tile] = part[:, side * HALF : (side + 1) * HALF]
    short_ref[...] = rows_ref[...].astype(bf16)
    g = lax.axis_index("chan")
    for place in range(BLOCKS):
        out_ref[place] = short_ref[4 * jnp.bitwise_xor(g, place % RUN) + place // (2 * RUN)]


def whole_sum(x):
    return jnp.sum(jnp.sum(x, axis=0, keepdims=True), axis=1, keepdims=True)


def seat():
    place, g = lax.axis_index("seq"), lax.axis_index("chan")
    owner = jnp.bitwise_xor(lax.rem(place, RUN), g)
    return g, owner, 4 * owner + place // (2 * RUN), lax.rem(place // RUN, 2)


def own_taps(taps_ref, channel):
    lane = lax.broadcasted_iota(jnp.int32, taps_ref.shape, 2)
    own = jnp.sum(jnp.where(lane == channel, taps_ref[...], 0.0), axis=2, keepdims=True)
    return [[own[b, j : j + 1, :] for j in range(TAPS)] for b in range(3)]


def unpack(data_ref, rows_ref, count):
    width = count // 2 * HALF
    rows_ref[:, :, :width] = data_ref[:, :, :width].astype(f32)
    parts = []
    for i in range(count):
        pieces = []
        for side in range(2):
            row, tile = place_of(2 * i + side)
            pieces.append(rows_ref[:, row, tile])
        parts.append(jnp.concatenate(pieces, axis=1))
    return parts


def mix(branch, taps):
    moved = [[x] + [later(x, j) for j in range(1, TAPS)] for x in branch]
    mixed = [
        taps[b][0] * moved[b][0] + taps[b][1] * moved[b][1] + taps[b][2] * moved[b][2]
        for b in range(3)
    ]
    return moved, mixed


def constants(strip_ref, turn_ref):
    left = strip_ref[: 2 * BLOCKS, : 3 * BLOCKS]
    right = strip_ref[2 * BLOCKS :, :]
    right = jnp.concatenate([right[:, :HALF], right], axis=1)
    last = 2 * BLOCKS
    odd = turn_ref[last : last + 1, :HALF], turn_ref[last : last + 1, HALF:]
    return left, right, (turn_ref[:BLOCKS, :], turn_ref[BLOCKS:last, :]), odd


def pair(values, i):
    re = values[2 * i * BLOCKS : (2 * i + 1) * BLOCKS]
    im = values[(2 * i + 1) * BLOCKS : (2 * i + 2) * BLOCKS]
    return re[:, :HALF], re[:, HALF:], im[:, :HALF], im[:, HALF:]


def spectra(signals, points, left, turn, odd):
    cosine, sine = turn
    odd_cos, odd_sin = odd
    start = dot_left(left, jnp.concatenate(signals, axis=1))
    stacked = []
    for i in range(len(signals)):
        re = start[:BLOCKS, i * SPAN : (i + 1) * SPAN]
        im = start[BLOCKS:, i * SPAN : (i + 1) * SPAN]
        re, im = re * cosine + im * sine, im * cosine - re * sine
        stacked += [re[:, :HALF] + re[:, HALF:], im[:, :HALF] + im[:, HALF:]]
        re, im = re[:, :HALF] - re[:, HALF:], im[:, :HALF] - im[:, HALF:]
        stacked += [re * odd_cos + im * odd_sin, im * odd_cos - re * odd_sin]
    values = dot_right(jnp.concatenate(stacked, axis=0), points)
    results = []
    for i in range(2 * len(signals)):
        re_cos, re_sin, im_cos, im_sin = pair(values, i)
        results.append((re_cos + im_sin, im_cos - re_sin))
    return [results[2 * i : 2 * i + 2] for i in range(len(signals))]


def times(a, b):
    return a[0] * b[0] - a[1] * b[1], a[0] * b[1] + a[1] * b[0]


def times_conj(a, b):
    return a[0] * b[0] + a[1] * b[1], a[1] * b[0] - a[0] * b[1]


def inverse(spectrums, points, right, turn, odd, b=None):
    cosine, sine = turn
    odd_cos, odd_sin = odd
    joined = [x for spectrum in spectrums for part in spectrum for x in part]
    back = dot_right(jnp.concatenate(joined, axis=0), points)
    turned = []
    for i in range(len(spectrums)):
        re_cos, re_sin, im_cos, im_sin = pair(back, 2 * i)
        even_re, even_im = re_cos - im_sin, im_cos + re_sin
        re_cos, re_sin, im_cos, im_sin = pair(back, 2 * i + 1)
        re, im = re_cos - im_sin, im_cos + re_sin
        re, im = re * odd_cos - im * odd_sin, im * odd_cos + re * odd_sin
        b_re = jnp.concatenate([even_re + re, even_re - re], axis=1)
        b_im = jnp.concatenate([even_im + im, even_im - im], axis=1)
        turned.append(
            jnp.concatenate([b_re * cosine - b_im * sine, b_im * cosine + b_re * sine], axis=0)
        )
    if b is not None:
        right = every_second_run(right.astype(f32), b).astype(bf16)
    return dot_left(right, jnp.concatenate(turned, axis=1))


def every_second_run(x, b):
    runs = [
        jnp.where(b == 0, x[first : first + RUN], x[first + RUN : first + 2 * RUN])
        for first in range(0, BLOCKS, 2 * RUN)
    ]
    return jnp.concatenate(runs, axis=0)


def corr_kernel(
    data_ref, taps_ref, skip_ref, points_ref, strip_ref, turn_ref, corr_ref, spec_ref, rows_ref
):
    g, owner, channel, b_own = seat()
    parts = unpack(data_ref, rows_ref, 4)
    taps = own_taps(taps_ref, channel)
    _, (query, key, value) = mix(parts[:3], taps)
    product, dw = key * value, parts[3] * query
    left, right, turn, odd = constants(strip_ref, turn_ref)
    points = points_ref[...]
    p, d = spectra([product, dw], points, left, turn, odd)
    for i, x in enumerate([x for spectrum in (p, d) for part in spectrum for x in part]):
        spec_ref[i * BLOCKS : (i + 1) * BLOCKS, :] = x
    b_there = jnp.where(is_far(g, owner), 1 - b_own, b_own)
    product_spec = [times_conj(d[e], p[e]) for e in range(2)]
    corr = inverse([product_spec], points, right, turn, odd, b_there)
    for side in range(2):
        corr_ref[side * FILTERS : (side + 1) * FILTERS, :] = corr[:, side * HALF : (side + 1) * HALF]


def channel_kernel(
    data_ref, taps_ref, skip_ref, points_ref, strip_ref, turn_ref, spec_ref, out_ref, rows_ref
):
    _, _, channel, b_own = seat()
    parts = unpack(data_ref, rows_ref, 6)
    grad, h = parts[3], parts[4] + parts[5]
    taps = own_taps(taps_ref, channel)
    lane = lax.broadcasted_iota(jnp.int32, (1, FILTERS), 1)
    line = skip_ref[...].reshape(1, FILTERS)
    direct = jnp.sum(jnp.where(lane == channel, line, 0.0), axis=1, keepdims=True)
    moved, (query, key, value) = mix(parts[:3], taps)
    product, dw = key * value, grad * query
    left, right, turn, odd = constants(strip_ref, turn_ref)
    points = points_ref[...]
    (h_spec,) = spectra([h], points, left, turn, odd)
    held = [spec_ref[i * BLOCKS : (i + 1) * BLOCKS, :] for i in range(8)]
    p = [(held[0], held[1]), (held[2], held[3])]
    d = [(held[4], held[5]), (held[6], held[7])]
    result = inverse(
        [
            [times(h_spec[e], p[e]) for e in range(2)],
            [times_conj(d[e], h_spec[e]) for e in range(2)],
        ],
        points,
        right,
        turn,
        odd,
    )
    conv_out = result[:, :SPAN] + direct * product
    dz = result[:, SPAN:] + direct * dw

    grads = [grad * conv_out, dz * value, dz * key]
    for b in range(3):
        g = grads[b]
        total = taps[b][0] * g + taps[b][1] * sooner(g, 1) + taps[b][2] * sooner(g, 2)
        mine = every_second_run(total, b_own)
        for side in range(2):
            out_ref[pl.ds(2 * b + side, FILTERS, stride=ROWS), :] = mine[
                :, side * HALF : (side + 1) * HALF
            ]
    for row in (6, 7):
        out_ref[pl.ds(row, FILTERS, stride=ROWS), :] = jnp.zeros((FILTERS, HALF), f32)
    sums = [whole_sum(grads[b] * moved[b][j]) for b in range(3) for j in range(TAPS)]
    sums.append(whole_sum(dw * product))
    lanes = lax.broadcasted_iota(jnp.int32, (1, HALF), 1)
    line = jnp.zeros((1, HALF), f32)
    for i, value in enumerate(sums):
        line = jnp.where(lanes == i, value, line)
    line = jnp.broadcast_to(line * TOTAL**-0.5, (FILTERS, HALF))
    out_ref[pl.ds(8, FILTERS, stride=ROWS), :] = line


def merge_kernel(answer_ref, corr_ref, out_ref):
    out_ref[...] = answer_ref[...]
    for side in range(2):
        out_ref[pl.ds(6 + side, FILTERS, stride=ROWS), :] = corr_ref[
            side * FILTERS : (side + 1) * FILTERS, :
        ]


def place_kernel(data_ref, grads_ref, skip_ref, short_ref, filter_ref, sums_ref):
    g = lax.axis_index("chan")
    for owner in range(GROUPS):
        first = ROWS * jnp.bitwise_xor(g, owner)
        rows = slice(4 * owner, 4 * owner + 4)
        for b in range(3):
            for side in range(2):
                grads_ref[b, rows, side * HALF : (side + 1) * HALF] = data_ref[
                    pl.ds(first + (2 * b + side), 4, stride=RUN * ROWS), :
                ]
        sums_ref[rows, :] = data_ref[pl.ds(first + 8, 4, stride=RUN * ROWS), :]
    padded = jnp.concatenate([sums_ref[...], jnp.zeros((HALF - FILTERS, HALF), f32)], axis=0)
    flipped = padded.T[:, :FILTERS]
    for b in range(3):
        short_ref[b] = flipped[TAPS * b : TAPS * (b + 1), :]
    skip_ref[...] = flipped[9:10, :]
    for x in range(4):
        for side in range(2):
            terms = data_ref[pl.ds(x * RUN * ROWS + 6 + side, RUN, stride=ROWS), :]
            total = jnp.sum(terms, axis=0, keepdims=True) * (TOTAL * GROUPS) ** -0.5
            filter_ref[x : x + 1, side * HALF : (side + 1) * HALF] = total


vmem = pl.BlockSpec(memory_space=pltpu.VMEM)
hbm = pl.BlockSpec(memory_space=pltpu.HBM)
params = pltpu.CompilerParams(vmem_limit_bytes=32 * 1024 * 1024)


def like(shape, dtype=f32):
    return jax.ShapeDtypeStruct(shape, dtype)


def body(inputs, short_weights, filters, skip, grad_out):
    points, strip, turn = [jnp.asarray(values) for values in tables()]
    message = pl.pallas_call(
        pack_kernel,
        out_shape=like((BLOCKS, 4, 3 * HALF), bf16),
        in_specs=[hbm] * 3,
        out_specs=vmem,
        scratch_shapes=[
            pltpu.VMEM((3, FILTERS, SPAN), bf16),
            pltpu.VMEM((FILTERS, SPAN), bf16),
            pltpu.VMEM((FILTERS, SPAN), f32),
            pltpu.VMEM((FILTERS, 4, 3 * HALF), f32),
            pltpu.VMEM((FILTERS, 4, 3 * HALF), bf16),
            pltpu.SemaphoreType.DMA((3,)),
        ],
        compiler_params=params,
    )(*[pltpu.with_memory_space_constraint(x, pltpu.HBM) for x in (inputs, grad_out, filters)])
    data = lax.all_to_all(message, "seq", split_axis=0, concat_axis=0, tiled=True)
    corr, spec = pl.pallas_call(
        corr_kernel,
        out_shape=(like((BLOCKS, HALF)), like((8 * BLOCKS, HALF))),
        in_specs=[vmem] * 6,
        out_specs=(vmem,) * 2,
        scratch_shapes=[pltpu.VMEM((BLOCKS, 4, 3 * HALF), f32)],
        compiler_params=params,
    )(data, short_weights, skip, points, strip, turn)
    corr = lax.ppermute(corr, ("seq", "chan"), owner_route())
    answer = pl.pallas_call(
        channel_kernel,
        out_shape=like((FILTERS * ROWS, HALF)),
        in_specs=[vmem] * 7,
        out_specs=vmem,
        scratch_shapes=[pltpu.VMEM((BLOCKS, 4, 3 * HALF), f32)],
        compiler_params=params,
        cost_estimate=pl.CostEstimate(flops=10**9, bytes_accessed=4 * 10**6, transcendentals=0),
    )(data, short_weights, skip, points, strip, turn, spec)
    answer = pl.pallas_call(
        merge_kernel,
        out_shape=like((FILTERS * ROWS, HALF)),
        in_specs=[vmem] * 2,
        out_specs=vmem,
        compiler_params=params,
    )(answer, corr)
    answer = lax.all_to_all(
        answer.reshape(FILTERS, 1, ROWS * HALF),
        "seq",
        split_axis=0,
        concat_axis=0,
        tiled=True,
        axis_index_groups=PARTNERS,
    ).reshape(FILTERS * ROWS, HALF)
    grads, skip_grad, short_grad, filter_grad = pl.pallas_call(
        place_kernel,
        out_shape=(
            like((3, FILTERS, SPAN)),
            like((1, FILTERS)),
            like((3, TAPS, FILTERS)),
            like((4, SPAN)),
        ),
        in_specs=[vmem],
        out_specs=(vmem,) * 4,
        scratch_shapes=[pltpu.VMEM((FILTERS, HALF), f32)],
        compiler_params=params,
    )(answer)
    return grads, filter_grad, skip_grad.reshape(FILTERS), short_grad


def solution(mesh):
    placed = (
        P(None, "chan", "seq"),
        P(None, None, "chan"),
        P(None, "seq"),
        P("chan"),
        P("chan", "seq"),
    )
    return jax.shard_map(
        body,
        mesh=mesh,
        in_specs=placed,
        out_specs=(P(None, "chan", "seq"), P("chan", "seq"), P("chan"), P(None, None, "chan")),
        check_vma=False,
    )
```
